32 devices in a mesh: section: 2 (over y), dp: 16 (over z, x, core).
Axes of the slice: x: 2, y: 2, z: 4, core: 2. Of those that a mesh axis runs over, the one named last changes fastest.
Arguments:
- boundary: bfloat16 [2, 4, 19840, 512], P('section', None, 'dp'), may hold values from -6 to 6
- entry_gain: float32 [2, 512], P('section'), may hold values from 0.25 to 1.75
- entry_shift: float32 [2, 512], P('section'), may hold values from -1.75 to 1.75
- widen_weight: bfloat16 [2, 512, 3072], P('section'), may hold values from -0.25 to 0.25
- hidden_bias: float32 [2, 3072], P('section'), may hold values from -1.75 to 1.75
- gate_gain: float32 [2, 1536], P('section'), may hold values from 0.25 to 1.75
- gate_shift: float32 [2, 1536], P('section'), may hold values from -1.75 to 1.75
- spatial_weight: bfloat16 [2, 324, 324], P('section'), may hold values from -0.4375 to 0.4375
- position_bias: float32 [2, 324], P('section'), may hold values from 0.5 to 1.5
- narrow_weight: bfloat16 [2, 1536, 512], P('section'), may hold values from -0.15625 to 0.15625
- output_bias: float32 [2, 512], P('section'), may hold values from -1.75 to 1.75
- crop_starts: int32 [2, 3], P('section'), may hold values from 0 to 224, as said below
Outputs:
- results: float32 [2, 4, 19840, 512], P('section', None, 'dp')
- entry_grads: float32 [2, 3, 512], P('section')
- widen_grad: float32 [2, 512, 3072], P('section')
- hidden_grads: float32 [2, 3072], P('section')
- gate_grads: float32 [2, 2, 1536], P('section')
- spatial_grad: float32 [2, 324, 324], P('section')
- position_grads: float32 [2, 324], P('section')
- narrow_grad: float32 [2, 1536, 512], P('section')
The draws below stay inside these ranges and needn't reach their ends.
Inputs may be any that keep to these rules, and one draw needn't show every extreme that they name: `crop_starts`: row l holds the starts of layer l's crops for images of 100, 196 and 324 patches; each crop lies inside the 324 x 324 weight, so the last start is 0.
All inputs are finite; a program needn't handle non-finite values.
Results may differ from the reference program's by a relative error of at most 0.01.
Values may be sent and summed in bfloat16 or wider, within the bound.
A program may use at most 448 MiB of HBM per device.

```python
import jax
import jax.numpy as jnp
from jax import lax

D = 512
FF = 3072
GATE = 1536
P_SMALL = 100
P_MID = 196
P_LARGE = 324
SETS = 2
MICRO = 4
ROWS_DEV = 1240
ROWS = 19840
N_DP = 16


def draw_crop_starts(key, part):
    key = jax.random.fold_in(key, 7)
    small_key, middle_key, pick_key = jax.random.split(key, 3)
    small = jax.random.randint(small_key, (2,), 0, P_LARGE - P_SMALL + 1)
    middle = jax.random.randint(middle_key, (2,), 0, P_LARGE - P_MID + 1)
    chosen = jax.random.randint(pick_key, (), 0, 2)
    small = jnp.where(jnp.arange(2) == chosen, P_LARGE - P_SMALL, small)
    return jnp.stack([small, middle, jnp.zeros((2,), jnp.int32)], axis=1).astype(jnp.int32)


def shard_levels(rng, extent, cuts, smallest, high):
    def one(axis_at, blocks):
        heights = jax.random.uniform(jax.random.fold_in(jax.random.fold_in(rng, 6), axis_at), (blocks,), jnp.float32, smallest / len(cuts), high / len(cuts))
        return jnp.repeat(jnp.exp(heights), extent[axis_at] // blocks).reshape((-1,) + (1,) * (len(extent) - axis_at - 1))

    level = one(*cuts[0])
    for cut in cuts[1:]:
        level = level * one(*cut)
    return level


def noise(own_key, shape, scale, bound, cuts=(), kind=jnp.bfloat16):
    entries = jax.random.normal(own_key, shape, jnp.float32) * scale
    if len(cuts) > 0:
        entries = shard_levels(own_key, shape, cuts, -0.22, 0.18) * entries
    return jnp.clip(entries, min=-bound, max=bound).astype(kind)


def setup_inputs(seed: int = 0) -> dict:
    splits = jax.random.split(jax.random.key(seed), 13)
    return {
        "boundary": noise(splits[0], (2, MICRO, ROWS, D), 1.0, 6.0, ((0, 2), (2, 16))),
        "entry_gain": jnp.clip(1.0 + 0.15 * jax.random.normal(splits[1], (2, D), jnp.float32), 0.25, 1.75),
        "entry_shift": noise(splits[2], (2, D), 0.3, 1.75, ((0, 2),), jnp.float32),
        "widen_weight": noise(splits[3], (2, D, FF), D ** -0.5, 0.25, ((0, 2),)),
        "hidden_bias": noise(splits[4], (2, FF), 0.3, 1.75, ((0, 2),), jnp.float32),
        "gate_gain": jnp.clip(1.0 + 0.15 * jax.random.normal(splits[5], (2, GATE), jnp.float32), 0.25, 1.75),
        "gate_shift": noise(splits[6], (2, GATE), 0.3, 1.75, ((0, 2),), jnp.float32),
        "spatial_weight": noise(splits[7], (2, P_LARGE, P_LARGE), P_MID ** -0.5, 0.4375, ((0, 2),)),
        "position_bias": jnp.clip(0.5 + 1.0 * jax.random.uniform(splits[8], (2, P_LARGE), jnp.float32) ** shard_levels(splits[8], (2, P_LARGE), ((0, 2),), -0.2, 0.2), 0.5, 1.5),
        "narrow_weight": noise(splits[9], (2, GATE, D), GATE ** -0.5, 0.15625, ((0, 2),)),
        "output_bias": noise(splits[10], (2, D), 0.3, 1.75, ((0, 2),), jnp.float32),
        "crop_starts": draw_crop_starts(jax.random.fold_in(splits[12], 71), 0),
    }


@jax.custom_vjp
def low(v):
    return lax.optimization_barrier(v.astype(jnp.bfloat16)).astype(jnp.float32)

@jax.custom_vjp
def low_back(v):
    return v

def low_keep(v):
    return (low(v), None)

def low_pass(kept, grad):
    return (grad,)

def back_keep(v):
    return (v, None)

def back_low(kept, grad):
    return (low(grad),)
low.defvjp(low_keep, low_pass)
low_back.defvjp(back_keep, back_low)
EPSILON = 1e-05
HIGHEST = lax.Precision.HIGHEST

def norm_rows(values, gain, shift):
    average = lax.optimization_barrier(jnp.mean(values, axis=-1, keepdims=True))
    centred = values - average
    spread = lax.optimization_barrier(jnp.mean(centred * centred, axis=-1, keepdims=True))
    return centred * lax.rsqrt(spread + EPSILON) * gain + shift

def smooth_gate(values):
    return 0.5 * values * (1.0 + jnp.tanh(0.7978845608028654 * (values + 0.044715 * values * values * values)))

def spatial_mix(gated, weight, bias, starts):
    pieces = []
    first = 0
    for index, count in enumerate((P_SMALL, P_MID, P_LARGE)):
        block = gated[first:first + SETS * count].reshape(SETS, count, gated.shape[-1])
        offset = starts[index]
        square = lax.dynamic_slice(weight, (offset, offset), (count, count))
        shift = lax.dynamic_slice(bias, (offset,), (count,))
        mixed = jnp.einsum('pq,sqc->spc', square, block, precision=HIGHEST) + shift[None, :, None]
        pieces.append(mixed.reshape(SETS * count, gated.shape[-1]))
        first = first + SETS * count
    return jnp.concatenate(pieces, axis=0)

def layer(inputs, params, starts):
    entry_gain, entry_shift, widen, hidden_bias, gate_gain, gate_shift, spatial, position, narrow, output_bias = params
    normed = low(norm_rows(inputs, entry_gain, entry_shift))
    hidden = low_back(jnp.dot(normed, widen, precision=HIGHEST) + hidden_bias)
    active = smooth_gate(hidden)
    half = active.shape[-1] // 2
    gated = low(norm_rows(active[:, half:], gate_gain, gate_shift))
    mixed = low_back(spatial_mix(gated, spatial, position, starts))
    product = low(active[:, :half] * mixed)
    branch = low_back(jnp.dot(product, narrow, precision=HIGHEST) + output_bias)
    return inputs + branch

def add_pair(left, right):
    return left + right

def pair_up(first, second):
    return jnp.stack([first, second])

def reference(boundary, entry_gain, entry_shift, widen_weight, hidden_bias, gate_gain, gate_shift, spatial_weight, position_bias, narrow_weight, output_bias, crop_starts):
    stacked = tuple((item.astype(jnp.float32) for item in (entry_gain, entry_shift, widen_weight, hidden_bias, gate_gain, gate_shift, spatial_weight, position_bias, narrow_weight, output_bias)))
    layer_one = tuple((item[0] for item in stacked))
    layer_two = tuple((item[1] for item in stacked))
    width = boundary.shape[-1]
    groups = MICRO * N_DP
    inputs = boundary[0].astype(jnp.float32).reshape(groups, ROWS_DEV, width)
    cotangent = boundary[1].astype(jnp.float32).reshape(groups, ROWS_DEV, width)

    def both_layers(first_rows, params_one, params_two):
        middle = layer(first_rows, params_one, crop_starts[0])
        passed = low_back(low(middle))
        return layer(passed, params_two, crop_starts[1])

    def one_group(totals, pair):
        first_rows, back_rows = pair
        outputs, pullback = jax.vjp(both_layers, first_rows, layer_one, layer_two)
        grad_rows, grad_one, grad_two = pullback(back_rows)
        return (jax.tree.map(add_pair, totals, (grad_one, grad_two)), (outputs, grad_rows))
    zeros = jax.tree.map(jnp.zeros_like, (layer_one, layer_two))
    totals, (outputs, grad_rows) = lax.scan(one_group, zeros, (inputs, cotangent))
    merged = jax.tree.map(pair_up, totals[0], totals[1])
    results = jnp.stack([grad_rows.reshape(MICRO, ROWS, width), outputs.reshape(MICRO, ROWS, width)])
    entry_grads = jnp.stack([merged[0], merged[1], merged[9]], axis=1)
    gate_grads = jnp.stack([merged[4], merged[5]], axis=1)
    return (results, entry_grads, merged[2], merged[3], gate_grads, merged[6], merged[7], merged[8])
```

```python
import jax
import jax.numpy as jnp
from jax import lax
from jax.experimental import pallas as pl
from jax.experimental.pallas import tpu as pltpu
from jax.sharding import PartitionSpec as P

P_SMALL = 100
P_MID = 196
P_LARGE = 324
EPSILON = 1e-05
BF = jnp.bfloat16
F32 = jnp.float32
MESH = pl.DeviceIdType.MESH
TILE = 256

HALVES = (
    {"first": 0, "rows": 592, "deep": 640, "starts": (0, 192, 384), "win": 208, "wide": 256, "out": 592},
    {"first": 592, "rows": 656, "deep": 768, "starts": (0, 320), "win": 336, "wide": 384, "out": 648},
)
PADDED = 1248
TALL = 768
ONES = 16


def dot(a, b):
    return lax.dot_general(a, b, (((1,), (0,)), ((), ())), preferred_element_type=F32)


def dot_nt(a, b):
    return lax.dot_general(a, b, (((1,), (1,)), ((), ())), preferred_element_type=F32)


def over_rows(rows, step, body):
    def one(index, carry):
        body(pl.multiple_of(index * step, step), step)
        return carry

    lax.fori_loop(0, rows // step, one, 0)
    if rows % step:
        body(rows - rows % step, rows % step)


def over_tiles(count, body):
    def one(index, carry):
        body(pl.multiple_of(index * TILE, TILE))
        return carry

    lax.fori_loop(0, count, one, 0)


def fold8(values):
    rows = values.shape[0]
    total = values[0:8]
    for at in range(8, rows, 8):
        total = total + values[at : at + 8]
    return total


def assemble(parts, starts, rows):
    pieces = []
    win = parts[0].shape[0]
    for index, (part, start) in enumerate(zip(parts, starts)):
        low = 0
        if index > 0:
            low = starts[index - 1] + win - start
            pieces.append(parts[index - 1][win - low :] + part[:low])
        high = win if index == len(parts) - 1 else starts[index + 1] - start
        pieces.append(part[low:high])
    return jnp.concatenate(pieces, axis=0)


def layer_kernel(
    bnd_ref,
    widen_ref,
    narrow_ref,
    sp_a,
    sp_b,
    spt_a,
    spt_b,
    pos_a,
    pos_b,
    eg_ref,
    es_ref,
    hb_ref,
    gg_ref,
    gs_ref,
    ob_ref,
    res_ref,
    wg_ref,
    ng_ref,
    ga_ref,
    gb_ref,
    pa_ref,
    pb_ref,
    gate_ref,
    entry_ref,
    buf,
    n_s,
    nt_s,
    g_s,
    gt_s,
    u_s,
    du_s,
    s_s,
    m_s,
    q_s,
    z_s,
    dv_s,
    wide_s,
    gsp_s,
    gh_s,
    o32,
    stage,
    load_sem,
    send_sem,
    recv_sem,
    out_sem,
):
    section = lax.axis_index("section")
    is_first = section == 0
    partner = {"section": 1 - section}
    micro = bnd_ref.shape[0]
    width = widen_ref.shape[0]
    gate = narrow_ref.shape[0]
    tiles = gate // TILE
    sp = (sp_a, sp_b)
    spt = (spt_a, spt_b)
    pos = (pos_a, pos_b)
    gsp = (ga_ref, gb_ref)
    psum = (pa_ref, pb_ref)

    def load(index, half):
        span = pl.ds(HALVES[half]["first"], HALVES[half]["rows"])
        return pltpu.make_async_copy(
            bnd_ref.at[index, span], buf.at[0, index, span], load_sem.at[index, half]
        )

    def send(index, half):
        span = pl.ds(HALVES[half]["first"], HALVES[half]["rows"])
        return pltpu.make_async_remote_copy(
            src_ref=stage.at[half, pl.ds(0, HALVES[half]["rows"])],
            dst_ref=buf.at[1, index, span],
            send_sem=send_sem.at[index, half],
            recv_sem=recv_sem.at[index, half],
            device_id=partner,
            device_id_type=MESH,
        )

    def store(index, half):
        count = HALVES[half]["out"]
        return pltpu.make_async_copy(
            o32.at[half, pl.ds(0, count)],
            res_ref.at[index, pl.ds(HALVES[half]["first"], count)],
            out_sem.at[half],
        )

    barrier = pltpu.get_barrier_semaphore()
    pl.semaphore_signal(barrier, inc=1, device_id=partner, device_id_type=MESH)

    for index in range(micro):
        for half in range(2):
            load(index, half).start()

    def clear(ref):
        rows = ref.shape[-2]

        def body(at, size):
            ref[pl.ds(at, size), :] = jnp.zeros((size, ref.shape[-1]), ref.dtype)

        over_rows(rows, 16, body)

    for ref in (wg_ref, ng_ref, pa_ref, pb_ref, n_s, g_s, m_s, q_s, gsp_s, gh_s):
        clear(ref)
    for ref in (ga_ref, gb_ref, gate_ref, entry_ref):
        ref[...] = jnp.zeros(ref.shape, ref.dtype)

    pl.semaphore_wait(barrier, 1)

    def forward(step, index, half):
        spec = HALVES[half]
        first, rows = spec["first"], spec["rows"]

        def entry(at, size):
            x = buf[section, index, pl.ds(first + at, size), :].astype(F32)
            centred = x - jnp.mean(x, axis=-1, keepdims=True)
            spread = jnp.mean(centred * centred, axis=-1, keepdims=True)
            normed = centred * lax.rsqrt(spread + EPSILON) * eg_ref[...] + es_ref[...]
            n_s[pl.ds(at, size), :] = normed.astype(BF)

        over_rows(rows, 16, entry)
        if spec["deep"] <= TALL and rows < HALVES[1]["rows"]:
            n_s[rows : spec["deep"], :] = jnp.zeros((spec["deep"] - rows, width), BF)

        def gelu_tile(at):
            hidden = dot(n_s[0:rows, :], widen_ref[:, pl.ds(at, TILE)]) + hb_ref[:, pl.ds(at, TILE)]
            square = hidden * hidden
            curve = jnp.tanh(hidden * (0.7978845608028654 + 0.035677408136300125 * square))
            above = curve + 1.0
            active = (0.5 * hidden) * above
            slope = above * (0.5 + (hidden - active) * (0.7978845608028654 + 0.10703222440890037 * square))
            return active, slope

        def lower(at):
            active, slope = gelu_tile(pl.multiple_of(gate + at, TILE))
            wide_s[0:rows, pl.ds(at, TILE)] = active
            dv_s[0:rows, pl.ds(at, TILE)] = slope.astype(BF)

        over_tiles(tiles, lower)

        def gate_norm(at, size):
            span = pl.ds(at, size)
            v = wide_s[span, :]
            centred = v - jnp.mean(v, axis=-1, keepdims=True)
            spread = jnp.mean(centred * centred, axis=-1, keepdims=True)
            factor = lax.rsqrt(spread + EPSILON)
            z = centred * factor
            z_s[span, :] = z.astype(BF)
            q_s[span, :] = (z * gg_ref[...] + gs_ref[...]).astype(BF)
            dv_s[span, :] = (dv_s[span, :].astype(F32) * factor).astype(BF)

        over_rows(rows, 16, gate_norm)

        def upper(at):
            active, slope = gelu_tile(at)
            u_s[0:rows, pl.ds(at, TILE)] = active.astype(BF)
            du_s[0:rows, pl.ds(at, TILE)] = slope.astype(BF)

        over_tiles(tiles, upper)

        def mix(at):
            parts = [
                dot(sp[half][w], q_s[start : start + spec["wide"], pl.ds(at, TILE)])
                for w, start in enumerate(spec["starts"])
            ]
            mixed = assemble(parts, spec["starts"], rows)
            shift = pos[half][...]
            mixed = mixed + jnp.concatenate([shift, shift], axis=1)
            s_s[0:rows, pl.ds(at, TILE)] = mixed.astype(BF)
            u = u_s[0:rows, pl.ds(at, TILE)].astype(F32)
            m_s[0:rows, pl.ds(at, TILE)] = (u * mixed).astype(BF)

        over_tiles(tiles, mix)

        @pl.when(step < micro)
        def _():
            @pl.when(jnp.logical_and(section == 1, step > 0))
            def _():
                store(index - 1, half).wait()

            @pl.when(jnp.logical_and(is_first, step > 0))
            def _():
                send(index - 1, half).wait_send()

            def project(at):
                x = buf[section, index, first : first + rows, pl.ds(at, TILE)].astype(F32)
                y = dot(m_s[0:rows, :], narrow_ref[:, pl.ds(at, TILE)])
                y = x + (y + ob_ref[:, pl.ds(at, TILE)])

                @pl.when(section == 1)
                def _():
                    o32[half, 0:rows, pl.ds(at, TILE)] = y

                @pl.when(is_first)
                def _():
                    stage[half, 0:rows, pl.ds(at, TILE)] = y.astype(BF)

            over_tiles(width // TILE, project)

            @pl.when(section == 1)
            def _():
                store(index, half).start()

            @pl.when(is_first)
            def _():
                send(index, half).start()

    def backward(step, index, half):
        spec = HALVES[half]
        first, rows, deep = spec["first"], spec["rows"], spec["deep"]
        other = 1 - section

        def cotangent(at, size):
            g = buf[other, index, pl.ds(first + at, size), :]
            g_s[pl.ds(at, size), :] = g
            entry_ref[2] += fold8(g.astype(F32))

        over_rows(rows, 16, cotangent)
        if rows < HALVES[1]["rows"]:
            g_s[rows:deep, :] = jnp.zeros((deep - rows, width), BF)
        gt_s[:, 0:deep] = g_s[0:deep, :].T
        nt_s[0:width, 0:deep] = n_s[0:deep, :].T
        lane = lax.broadcasted_iota(jnp.int32, (ONES, deep), 1)
        nt_s[width : width + ONES, 0:deep] = jnp.where(lane < rows, 1.0, 0.0).astype(BF)

        def narrow_total(at):
            ng_ref[:, pl.ds(at, TILE)] += dot(gt_s[:, 0:deep], m_s[0:deep, pl.ds(at, TILE)])

        over_tiles(tiles, narrow_total)

        def split(at):
            span = pl.ds(at, TILE)
            gm = dot_nt(g_s[0:rows, :], narrow_ref[span, :])
            moved = (gm * u_s[0:rows, span].astype(F32)).astype(BF)
            gsp_s[0:rows, span] = moved
            moved = moved.astype(F32)
            psum[half][...] += moved[:, 0:128] + moved[:, 128:256]
            mixed = s_s[0:rows, span].astype(F32)
            gh_s[0:rows, span] = (gm * mixed * du_s[0:rows, span].astype(F32)).astype(BF)

        over_tiles(tiles, split)

        def unmix(at):
            parts = [
                dot(spt[half][w], gsp_s[start : start + spec["wide"], pl.ds(at, TILE)])
                for w, start in enumerate(spec["starts"])
            ]
            wide_s[0:rows, pl.ds(at, TILE)] = assemble(parts, spec["starts"], rows)

        over_tiles(tiles, unmix)

        for w, start in enumerate(spec["starts"]):
            gsp[half][w] += dot_nt(
                gsp_s[start : start + spec["win"], :], q_s[start : start + spec["wide"], :]
            )

        def gate_back(at, size):
            span = pl.ds(at, size)
            gq = wide_s[span, :]
            z = z_s[span, :].astype(F32)
            gate_ref[0] += fold8(gq * z)
            gate_ref[1] += fold8(gq)
            e = gq * gg_ref[...]
            first_mean = jnp.mean(e, axis=-1, keepdims=True)
            second_mean = jnp.mean(e * z, axis=-1, keepdims=True)
            gv = (e - first_mean - z * second_mean) * dv_s[span, :].astype(F32)
            gh_s[span, gate : 2 * gate] = gv.astype(BF)

        over_rows(rows, 16, gate_back)

        def widen_total(at):
            wg_ref[:, pl.ds(at, TILE)] += dot(nt_s[:, 0:deep], gh_s[0:deep, pl.ds(at, TILE)])

        over_tiles(2 * tiles, widen_total)

        def pull(at):
            wide_s[0:rows, pl.ds(at, TILE)] = dot_nt(
                gh_s[0:rows, :], widen_ref[pl.ds(at, TILE), :]
            )

        over_tiles(width // TILE, pull)

        def entry_back(at, size):
            span = pl.ds(at, size)
            x = buf[section, index, pl.ds(first + at, size), :].astype(F32)
            centred = x - jnp.mean(x, axis=-1, keepdims=True)
            spread = jnp.mean(centred * centred, axis=-1, keepdims=True)
            factor = lax.rsqrt(spread + EPSILON)
            z = centred * factor
            gn = wide_s[span, 0:width]
            entry_ref[0] += fold8(gn * z)
            entry_ref[1] += fold8(gn)
            e = gn * eg_ref[...]
            first_mean = jnp.mean(e, axis=-1, keepdims=True)
            second_mean = jnp.mean(e * z, axis=-1, keepdims=True)
            back = factor * (e - first_mean - z * second_mean)
            gy = buf[other, index, pl.ds(first + at, size), :].astype(F32)
            return span, gy + back

        @pl.when(is_first)
        def _():
            @pl.when(step > micro)
            def _():
                store(index - 1, half).wait()

            def keep(at, size):
                span, gx = entry_back(at, size)
                o32[half, span, :] = gx

            over_rows(rows, 16, keep)
            store(index, half).start()

        @pl.when(section == 1)
        def _():
            @pl.when(step > 0)
            def _():
                send(index - 1, half).wait_send()

            def keep(at, size):
                span, gx = entry_back(at, size)
                stage[half, span, :] = gx.astype(BF)

            over_rows(rows, 16, keep)
            send(index, half).start()

    def one_step(step, carry):
        index = lax.rem(step, micro)
        for half in range(2):

            @pl.when(step < micro)
            def _():
                load(index, half).wait()

            @pl.when(section == 1)
            def _():
                send(index, half).wait_recv()

            forward(step, index, half)

            @pl.when(jnp.logical_and(is_first, step >= micro))
            def _():
                send(index, half).wait_recv()

            @pl.when(jnp.logical_or(section == 1, step >= micro))
            def _():
                backward(step, index, half)

        return carry

    lax.fori_loop(0, micro * (2 - section), one_step, 0)

    for half in range(2):
        store(micro - 1, half).wait()
        send(micro - 1, half).wait_send()


def place(square, offset, rows, columns):
    count = square.shape[0]
    return jnp.pad(square, ((offset, rows - offset - count), (offset, columns - offset - count)))


def windows(squares):
    small, middle, large = squares
    first = place(small, 0, 208, 256) + place(small, P_SMALL, 208, 256)
    return (
        jnp.stack([first, place(middle, 8, 208, 256), place(middle, 12, 208, 256)]),
        jnp.stack([place(large, 0, 336, 384), place(large, 4, 336, 384)]),
    )


def shards(
    boundary,
    entry_gain,
    entry_shift,
    widen_weight,
    hidden_bias,
    gate_gain,
    gate_shift,
    spatial_weight,
    position_bias,
    narrow_weight,
    output_bias,
    crop_starts,
):
    micro, rows_dev, width = boundary.shape[1:]
    hidden = widen_weight.shape[-1]
    gate = hidden // 2
    starts = crop_starts[0]
    spatial = spatial_weight[0]
    position = position_bias[0]
    bnd = jnp.pad(boundary[0], ((0, 0), (0, PADDED - rows_dev), (0, 0)))
    counts = (P_SMALL, P_MID, P_LARGE)
    squares = [
        lax.dynamic_slice(spatial, (starts[k], starts[k]), (c, c)) for k, c in enumerate(counts)
    ]
    shifts = [lax.dynamic_slice(position, (starts[k],), (c,)) for k, c in enumerate(counts)]
    sp_a, sp_b = windows(squares)
    spt_a, spt_b = windows([item.T for item in squares])
    pos_a = jnp.concatenate([shifts[0], shifts[0], shifts[1], shifts[1]])
    pos_b = jnp.pad(jnp.concatenate([shifts[2], shifts[2]]), (0, 8))
    pos_a = jnp.broadcast_to(pos_a[:, None], (592, 128))
    pos_b = jnp.broadcast_to(pos_b[:, None], (656, 128))

    vmem = pl.BlockSpec(memory_space=pltpu.VMEM)
    anywhere = pl.BlockSpec(memory_space=pl.ANY)
    most = HALVES[1]["rows"]
    outs = pl.pallas_call(
        layer_kernel,
        out_shape=(
            jax.ShapeDtypeStruct((micro, rows_dev, width), F32),
            jax.ShapeDtypeStruct((width + ONES, hidden), F32),
            jax.ShapeDtypeStruct((width, gate), F32),
            jax.ShapeDtypeStruct((3, 208, 256), F32),
            jax.ShapeDtypeStruct((2, 336, 384), F32),
            jax.ShapeDtypeStruct((592, 128), F32),
            jax.ShapeDtypeStruct((656, 128), F32),
            jax.ShapeDtypeStruct((2, 8, gate), F32),
            jax.ShapeDtypeStruct((3, 8, width), F32),
        ),
        in_specs=[anywhere] + [vmem] * 14,
        out_specs=[anywhere] + [vmem] * 8,
        scratch_shapes=[
            pltpu.VMEM((2, micro, PADDED, width), BF),
            pltpu.VMEM((TALL, width), BF),
            pltpu.VMEM((width + ONES, TALL), BF),
            pltpu.VMEM((TALL, width), BF),
            pltpu.VMEM((width, TALL), BF),
            pltpu.VMEM((most, gate), BF),
            pltpu.VMEM((most, gate), BF),
            pltpu.VMEM((most, gate), BF),
            pltpu.VMEM((TALL, gate), BF),
            pltpu.VMEM((704, gate), BF),
            pltpu.VMEM((most, gate), BF),
            pltpu.VMEM((most, gate), BF),
            pltpu.VMEM((most, gate), F32),
            pltpu.VMEM((704, gate), BF),
            pltpu.VMEM((TALL, hidden), BF),
            pltpu.VMEM((2, most, width), F32),
            pltpu.VMEM((2, most, width), BF),
            pltpu.SemaphoreType.DMA((micro, 2)),
            pltpu.SemaphoreType.DMA((micro, 2)),
            pltpu.SemaphoreType.DMA((micro, 2)),
            pltpu.SemaphoreType.DMA((2,)),
        ],
        compiler_params=pltpu.CompilerParams(
            collective_id=0, has_side_effects=True, vmem_limit_bytes=63 * 2**20
        ),
        name="layer_relay",
    )(
        bnd,
        widen_weight[0],
        narrow_weight[0],
        sp_a,
        sp_b,
        spt_a,
        spt_b,
        pos_a,
        pos_b,
        entry_gain,
        entry_shift,
        hidden_bias,
        gate_gain,
        gate_shift,
        output_bias,
    )
    results, wide_total, narrow_total, square_a, square_b, line_a, line_b, gate_total, entry_total = outs

    spatial_total = jnp.zeros(spatial.shape, F32)
    position_total = jnp.zeros(position.shape, F32)
    line_a = jnp.sum(line_a, axis=1)
    line_b = jnp.sum(line_b, axis=1)
    square_parts = (
        square_a[0, :100, :100] + square_a[0, 100:200, 100:200],
        square_a[1, 8:204, 8:204] + square_a[2, 12:208, 12:208],
        square_b[0, :324, :324] + square_b[1, 4:328, 4:328],
    )
    line_parts = (
        line_a[0:100] + line_a[100:200],
        line_a[200:396] + line_a[396:592],
        line_b[0:324] + line_b[324:648],
    )
    for k, c in enumerate(counts):
        at = (starts[k], starts[k])
        current = lax.dynamic_slice(spatial_total, at, (c, c))
        spatial_total = lax.dynamic_update_slice(spatial_total, current + square_parts[k], at)
        current = lax.dynamic_slice(position_total, (starts[k],), (c,))
        position_total = lax.dynamic_update_slice(position_total, current + line_parts[k], (starts[k],))
    small = jnp.concatenate(
        [
            jnp.sum(entry_total, axis=1).reshape(-1),
            wide_total[width],
            jnp.sum(gate_total, axis=1).reshape(-1),
            position_total,
        ]
    )
    wide_total, narrow_total, spatial_total, small = lax.psum(
        (wide_total[:width], narrow_total, spatial_total, small), "dp"
    )
    at = 3 * width
    entry_grads = small[:at].reshape(3, width)
    hidden_grads = small[at : at + hidden]
    at = at + hidden
    gate_grads = small[at : at + 2 * gate].reshape(2, gate)
    position_total = small[at + 2 * gate :]
    return (
        results[None],
        entry_grads[None],
        wide_total[None],
        hidden_grads[None],
        gate_grads[None],
        spatial_total[None],
        position_total[None],
        narrow_total.T[None],
    )


def solution(mesh):
    placed = (
        P("section", None, "dp", None),
        P("section", None),
        P("section", None),
        P("section", None, None),
        P("section", None),
        P("section", None),
        P("section", None),
        P("section", None, None),
        P("section", None),
        P("section", None, None),
        P("section", None),
        P("section", None),
    )
    return jax.shard_map(
        shards,
        mesh=mesh,
        in_specs=placed,
        out_specs=(
            P("section", None, "dp", None),
            P("section", None, None),
            P("section", None, None),
            P("section", None),
            P("section", None, None),
            P("section", None, None),
            P("section", None),
            P("section", None, None),
        ),
        check_vma=False,
    )
```

```python
import jax
import jax.numpy as jnp
from jax import lax
from jax.experimental import pallas as pl
from jax.experimental.pallas import tpu as pltpu
from jax.sharding import PartitionSpec as P

P_SMALL = 100
P_MID = 196
P_LARGE = 324
EPSILON = 1e-05
BF = jnp.bfloat16
F32 = jnp.float32
MESH = pl.DeviceIdType.MESH
TILE = 256

HALVES = (
    {"first": 0, "rows": 592, "deep": 640, "starts": (0, 192, 384), "win": 208, "wide": 256, "out": 592},
    {"first": 592, "rows": 656, "deep": 768, "starts": (0, 320), "win": 336, "wide": 384, "out": 648},
)
PADDED = 1248
TALL = 768
PART = 32
NARROW_AT = 528
SMALL_AT = 784
SMALL = 112
PACKED = 896
CHUNKS = 7
ONES = 16


def dot(a, b):
    return lax.dot_general(a, b, (((1,), (0,)), ((), ())), preferred_element_type=F32)


def dot_nt(a, b):
    return lax.dot_general(a, b, (((1,), (1,)), ((), ())), preferred_element_type=F32)


def over_rows(rows, step, body, part=None):
    if part is not None:
        inner = body

        def body(at, size):
            for low in range(0, size, part):
                inner(at + low, min(part, size - low))

    def one(index, carry):
        body(pl.multiple_of(index * step, step), step)
        return carry

    if rows // step == 1:
        body(0, step)
    else:
        lax.fori_loop(0, rows // step, one, 0)
    if rows % step:
        body(rows - rows % step, rows % step)


def over_tiles(count, body):
    def one(index, carry):
        body(pl.multiple_of(index * TILE, TILE))
        return carry

    lax.fori_loop(0, count, one, 0)


def fold8(values):
    rows = values.shape[0]
    total = values[0:8]
    for at in range(8, rows, 8):
        total = total + values[at : at + 8]
    return total


def assemble(parts, starts, rows):
    pieces = []
    win = parts[0].shape[0]
    for index, (part, start) in enumerate(zip(parts, starts)):
        low = 0
        if index > 0:
            low = starts[index - 1] + win - start
            pieces.append(parts[index - 1][win - low :] + part[:low])
        high = win if index == len(parts) - 1 else starts[index + 1] - start
        pieces.append(part[low:high])
    return jnp.concatenate(pieces, axis=0)


class Work:
    def __init__(self, names, refs):
        for name, ref in zip(names, refs):
            setattr(self, name, ref)


INPUTS = (
    "bnd", "widen", "narrow", "sp_a", "sp_b", "spt_a", "spt_b", "pos_a", "pos_b",
    "eg", "es", "hb", "gg", "gs", "ob",
)
OUTPUTS = ("res", "packed")
SCRATCH = (
    "wg", "ng", "ga", "gb", "pa", "pb", "gate_sum", "entry_sum",
    "buf", "n", "nt", "g", "gt", "u", "s", "m", "q", "z", "wide", "gh",
    "stage", "kept", "load_sem", "send_sem", "recv_sem", "out_sem",
    "ready", "across_send", "across_recv", "around_send", "around_recv", "own_sem",
)


def row_stats(x):
    centred = x - jnp.mean(x, axis=-1, keepdims=True)
    spread = jnp.mean(centred * centred, axis=-1, keepdims=True)
    return centred, lax.rsqrt(spread + EPSILON)


def entry_norm(w, half, x_at):
    spec = HALVES[half]

    def body(at, size):
        centred, factor = row_stats(x_at(at, size).astype(F32))
        w.n[pl.ds(at, size), :] = (centred * factor * w.eg[...] + w.es[...]).astype(BF)

    over_rows(spec["rows"], 336, body, PART)
    if spec["rows"] < HALVES[1]["rows"]:
        w.n[spec["rows"] : spec["deep"], :] = jnp.zeros((spec["deep"] - spec["rows"], w.n.shape[1]), BF)


def gelu_tile(w, rows, at):
    hidden = dot(w.n[0:rows, :], w.widen[:, pl.ds(at, TILE)]) + w.hb[:, pl.ds(at, TILE)]
    square = hidden * hidden
    curve = jnp.tanh(hidden * (0.7978845608028654 + 0.035677408136300125 * square))
    above = curve + 1.0
    active = (0.5 * hidden) * above
    slope = above * (0.5 + (hidden - active) * (0.7978845608028654 + 0.10703222440890037 * square))
    return active, slope


def lower_half(w, half):
    rows, gate = HALVES[half]["rows"], w.narrow.shape[0]

    def body(at):
        active, slope = gelu_tile(w, rows, pl.multiple_of(gate + at, TILE))
        w.wide[0:rows, pl.ds(at, TILE)] = active
        w.gh[0:rows, pl.ds(pl.multiple_of(gate + at, TILE), TILE)] = slope.astype(BF)

    over_tiles(gate // TILE, body)


def gate_norm(w, half):
    gate = w.narrow.shape[0]

    def body(at, size):
        span = pl.ds(at, size)
        centred, factor = row_stats(w.wide[span, :])
        z = centred * factor
        w.z[span, :] = z.astype(BF)
        w.q[span, :] = (z * w.gg[...] + w.gs[...]).astype(BF)
        w.gh[span, gate:] = (w.gh[span, gate:].astype(F32) * factor).astype(BF)

    over_rows(HALVES[half]["rows"], 336, body, PART)


def upper_half(w, half):
    rows, gate = HALVES[half]["rows"], w.narrow.shape[0]

    def body(at):
        active, slope = gelu_tile(w, rows, at)
        w.u[0:rows, pl.ds(at, TILE)] = active.astype(BF)
        w.gh[0:rows, pl.ds(at, TILE)] = slope.astype(BF)

    over_tiles(gate // TILE, body)


def mix(w, half):
    spec, gate = HALVES[half], w.narrow.shape[0]
    rows = spec["rows"]
    square, shift = (w.sp_a, w.sp_b)[half], (w.pos_a, w.pos_b)[half]

    def body(at):
        span = pl.ds(at, TILE)
        parts = [
            dot(square[i], w.q[start : start + spec["wide"], span])
            for i, start in enumerate(spec["starts"])
        ]
        line = shift[...]
        mixed = assemble(parts, spec["starts"], rows) + jnp.concatenate([line, line], axis=1)
        w.s[0:rows, span] = mixed.astype(BF)
        w.m[0:rows, span] = (w.u[0:rows, span].astype(F32) * mixed).astype(BF)

    over_tiles(gate // TILE, body)


def project(w, half, x_at, keep):
    rows = HALVES[half]["rows"]

    def body(at):
        span = pl.ds(at, TILE)
        y = dot(w.m[0:rows, :], w.narrow[:, span])
        keep(span, x_at(0, rows, span).astype(F32) + (y + w.ob[:, span]))

    over_tiles(w.narrow.shape[1] // TILE, body)


def cotangent(w, half, gy_at):
    spec = HALVES[half]
    rows, deep, width = spec["rows"], spec["deep"], w.narrow.shape[1]

    def body(at, size):
        g = gy_at(at, size)
        w.g[pl.ds(at, size), :] = g
        w.entry_sum[2] += fold8(g.astype(F32))

    over_rows(rows, rows, body)
    if rows < HALVES[1]["rows"]:
        w.g[rows:deep, :] = jnp.zeros((deep - rows, width), BF)
    w.gt[:, 0:deep] = w.g[0:deep, :].T
    w.nt[0:width, 0:deep] = w.n[0:deep, :].T
    lane = lax.broadcasted_iota(jnp.int32, (ONES, deep), 1)
    w.nt[width : width + ONES, 0:deep] = jnp.where(lane < rows, 1.0, 0.0).astype(BF)


def narrow_total(w, half):
    deep = HALVES[half]["deep"]

    def body(at):
        span = pl.ds(at, TILE)
        w.ng[:, span] += dot(w.gt[:, 0:deep], w.m[0:deep, span])

    over_tiles(w.narrow.shape[0] // TILE, body)


def split(w, half):
    rows = HALVES[half]["rows"]
    line = (w.pa, w.pb)[half]

    def body(at):
        span = pl.ds(at, TILE)
        gm = dot_nt(w.g[0:rows, :], w.narrow[span, :])
        moved = (gm * w.u[0:rows, span].astype(F32)).astype(BF)
        mixed = w.s[0:rows, span].astype(F32)
        w.s[0:rows, span] = moved
        moved = moved.astype(F32)
        line[...] += moved[:, 0:128] + moved[:, 128:256]
        w.gh[0:rows, span] = (gm * mixed * w.gh[0:rows, span].astype(F32)).astype(BF)

    over_tiles(w.narrow.shape[0] // TILE, body)


def unmix(w, half):
    spec = HALVES[half]
    square = (w.spt_a, w.spt_b)[half]

    def body(at):
        span = pl.ds(at, TILE)
        parts = [
            dot(square[i], w.s[start : start + spec["wide"], span])
            for i, start in enumerate(spec["starts"])
        ]
        w.wide[0 : spec["rows"], span] = assemble(parts, spec["starts"], spec["rows"])

    over_tiles(w.narrow.shape[0] // TILE, body)


def spatial_total(w, half):
    spec = HALVES[half]
    total = (w.ga, w.gb)[half]
    for i, start in enumerate(spec["starts"]):
        total[i] += dot_nt(w.s[start : start + spec["win"], :], w.q[start : start + spec["wide"], :])


def gate_back(w, half):
    gate = w.narrow.shape[0]

    def body(at, size):
        span = pl.ds(at, size)
        gq = w.wide[span, :]
        z = w.z[span, :].astype(F32)
        w.gate_sum[0] += fold8(gq * z)
        w.gate_sum[1] += fold8(gq)
        e = gq * w.gg[...]
        first_mean = jnp.mean(e, axis=-1, keepdims=True)
        second_mean = jnp.mean(e * z, axis=-1, keepdims=True)
        gv = (e - first_mean - z * second_mean) * w.gh[span, gate:].astype(F32)
        w.gh[span, gate : 2 * gate] = gv.astype(BF)

    over_rows(HALVES[half]["rows"], 336, body, PART)


def widen_total(w, half):
    deep = HALVES[half]["deep"]

    def body(at):
        span = pl.ds(at, TILE)
        w.wg[:, span] += dot(w.nt[:, 0:deep], w.gh[0:deep, span])

    over_tiles(w.widen.shape[1] // TILE, body)


def pull(w, half):
    rows = HALVES[half]["rows"]

    def body(at):
        w.wide[0:rows, pl.ds(at, TILE)] = dot_nt(w.gh[0:rows, :], w.widen[pl.ds(at, TILE), :])

    over_tiles(w.widen.shape[0] // TILE, body)


def entry_back(w, half, x_at, gy_at, keep):
    width = w.widen.shape[0]

    def body(at, size):
        span = pl.ds(at, size)
        centred, factor = row_stats(x_at(at, size).astype(F32))
        z = centred * factor
        gn = w.wide[span, 0:width]
        w.entry_sum[0] += fold8(gn * z)
        w.entry_sum[1] += fold8(gn)
        e = gn * w.eg[...]
        first_mean = jnp.mean(e, axis=-1, keepdims=True)
        second_mean = jnp.mean(e * z, axis=-1, keepdims=True)
        keep(span, gy_at(at, size).astype(F32) + factor * (e - first_mean - z * second_mean))

    over_rows(HALVES[half]["rows"], 336, body, PART)


def clear(ref):
    def body(at, size):
        ref[pl.ds(at, size), :] = jnp.zeros((size, ref.shape[-1]), ref.dtype)

    over_rows(ref.shape[-2], 32, body)


def clear_all(w):
    for ref in (w.wg, w.ng, w.pa, w.pb, w.n, w.g, w.m, w.q, w.s, w.gh):
        clear(ref)
    for ref in (w.ga, w.gb, w.gate_sum, w.entry_sum):
        ref[...] = jnp.zeros(ref.shape, ref.dtype)


class Group:
    def __init__(self):
        at = lax.axis_index("dp")
        self.core = lax.rem(at, 2)
        self.x = lax.rem(at // 2, 2)
        self.z = at // 4
        self.beside = {"dp": at + 1 - 2 * self.core}
        self.across = {"dp": at + 2 - 4 * self.x}
        self.far = [lax.rem(self.z + off, 4) for off in (1, 2, 3)]
        self.around = [{"dp": far * 4 + lax.rem(at, 4)} for far in self.far]
        self.everyone = [self.beside, self.across] + self.around


def turn(values, rows, lanes):
    if rows:
        values = pltpu.roll(values, values.shape[0] - rows, 0)
    if lanes:
        values = pltpu.roll(values, values.shape[1] - lanes, 1)
    return values


def pack(w):
    gate, width = w.narrow.shape
    w.wg[width + 1 : width + 2, 0:gate] = jnp.sum(w.gate_sum[0], axis=0, keepdims=True)
    w.wg[width + 1 : width + 2, gate:] = jnp.sum(w.gate_sum[1], axis=0, keepdims=True)
    for k in range(3):
        w.wg[width + 2 : width + 3, k * width : (k + 1) * width] = jnp.sum(
            w.entry_sum[k], axis=0, keepdims=True
        )
    clear(w.gh.at[SMALL_AT:PACKED])

    def body(at, size):
        w.gh[pl.ds(at, size), :] = w.wg[pl.ds(at, size), :].astype(BF)

    over_rows(w.wg.shape[0], 48, body)
    for b in range(6):
        w.gh[NARROW_AT:SMALL_AT, b * 512 : (b + 1) * 512] = w.ng[:, b * 256 : (b + 1) * 256].T.astype(BF)

    def put(block, lane, first):
        for b in range(0, block.shape[0], SMALL):
            rows = block[b : b + SMALL]
            at = (first + b // SMALL) * 512 + lane
            w.gh[SMALL_AT : SMALL_AT + rows.shape[0], at : at + rows.shape[1]] = rows.astype(BF)

    def with_line(block, line):
        sums = jnp.sum(line[0 : block.shape[0]], axis=1, keepdims=True)
        last = lax.broadcasted_iota(jnp.int32, block.shape, 1) == block.shape[1] - 1
        return jnp.where(last, sums, block)

    line_a, line_b = w.pa[...], w.pb[...]
    large = w.gb[0] + turn(w.gb[1], 4, 4)
    put(with_line(large, line_b + turn(line_b, 324, 0)), 0, 0)
    small = (w.ga[0] + turn(w.ga[0], P_SMALL, P_SMALL))[:, 0:128]
    put(with_line(small, line_a + turn(line_a, P_SMALL, 0)), 384, 0)
    middle = turn(w.ga[1], 8, 8) + turn(w.ga[2], 12, 12)
    put(with_line(middle, turn(line_a, 200, 0) + turn(line_a, 396, 0)), 0, 3)


def add_up(w, group):
    part = PACKED // 4 // CHUNKS
    wide = w.gh.shape[1]
    sides = ((w.m, 0), (w.q, wide // 2))
    quarter = wide // 4

    def rows_at(core, chunk, x):
        return pl.multiple_of(core * (PACKED // 2) + (2 * chunk + x) * part, 16)

    def remote(src, dst, send, recv, to):
        return pltpu.make_async_remote_copy(
            src_ref=src, dst_ref=dst, send_sem=send, recv_sem=recv, device_id=to, device_id_type=MESH
        )

    def halves(chunk, side):
        land, column = sides[side]
        return remote(
            w.gh.at[pl.ds(rows_at(1 - group.core, chunk, 0), 2 * part), pl.ds(column, wide // 2)],
            land.at[pl.ds(2 * chunk * part, 2 * part)],
            w.across_send.at[side, chunk],
            w.across_recv.at[side, chunk],
            group.beside,
        )

    def quarters(chunk, side):
        land, column = sides[side]
        return remote(
            w.gh.at[pl.ds(rows_at(group.core, chunk, 1 - group.x), part), pl.ds(column, wide // 2)],
            land.at[pl.ds(PACKED // 2 + chunk * part, part)],
            w.across_send.at[2 + side, chunk],
            w.across_recv.at[2 + side, chunk],
            group.across,
        )

    def column_of(z):
        return pl.ds(pl.multiple_of(z * quarter, 128), quarter)

    def landed(chunk, k):
        row = (k // 2) * (PACKED // 4) + chunk * part
        return w.z.at[pl.ds(row, part), pl.ds((k % 2) * quarter, quarter)]

    def shares(chunk, k):
        return remote(
            w.gh.at[pl.ds(rows_at(group.core, chunk, group.x), part), column_of(group.far[k])],
            landed(chunk, k),
            w.around_send.at[0, k, chunk],
            w.around_recv.at[0, k, chunk],
            group.around[k],
        )

    def total_of(chunk):
        return w.u.at[pl.ds(chunk * part, part), pl.ds(0, quarter)]

    def own_place(chunk):
        return w.packed.at[pl.ds(rows_at(group.core, chunk, group.x), part), column_of(group.z)]

    def back_around(chunk, k):
        return remote(
            total_of(chunk),
            own_place(chunk),
            w.around_send.at[1, k, chunk],
            w.around_recv.at[1, k, chunk],
            group.around[k],
        )

    def own(chunk):
        return pltpu.make_async_copy(total_of(chunk), own_place(chunk), w.own_sem.at[chunk])

    def back_across(chunk):
        span = pl.ds(rows_at(group.core, chunk, group.x), part)
        return remote(
            w.packed.at[span],
            w.packed.at[span],
            w.across_send.at[4, chunk],
            w.across_recv.at[4, chunk],
            group.across,
        )

    def back_beside(chunk):
        span = pl.ds(rows_at(group.core, chunk, 0), 2 * part)
        return remote(
            w.packed.at[span],
            w.packed.at[span],
            w.across_send.at[5, chunk],
            w.across_recv.at[5, chunk],
            group.beside,
        )

    def accumulate(at, side, row, size):
        land, column = sides[side]
        rows, columns = pl.ds(at, size), pl.ds(column, wide // 2)
        total = w.gh[rows, columns].astype(F32) + land[row : row + size, :].astype(F32)
        w.gh[rows, columns] = total.astype(BF)

    for chunk in range(CHUNKS):
        for side in range(2):
            halves(chunk, side).start()
    for chunk in range(CHUNKS):
        for side in range(2):
            halves(chunk, side).wait_recv()
            accumulate(rows_at(group.core, chunk, 0), side, 2 * chunk * part, 2 * part)
            quarters(chunk, side).start()
    for chunk in range(CHUNKS):
        for side in range(2):
            quarters(chunk, side).wait_recv()
            accumulate(rows_at(group.core, chunk, group.x), side, PACKED // 2 + chunk * part, part)
        for k in range(3):
            shares(chunk, k).start()
    for chunk in range(CHUNKS):
        total = w.gh[pl.ds(rows_at(group.core, chunk, group.x), part), column_of(group.z)].astype(F32)
        for k in range(3):
            shares(chunk, k).wait_recv()
            total = total + landed(chunk, k)[...].astype(F32)
        total_of(chunk)[...] = total.astype(BF)
        own(chunk).start()
        for k in range(3):
            back_around(chunk, k).start()
    for chunk in range(CHUNKS):
        own(chunk).wait()
        for k in range(3):
            back_around(chunk, k).wait_recv()
        back_across(chunk).start()
    for chunk in range(CHUNKS):
        back_across(chunk).wait_recv()
        back_beside(chunk).start()
    for chunk in range(CHUNKS):
        back_beside(chunk).wait_recv()
    for chunk in range(CHUNKS):
        for side in range(2):
            halves(chunk, side).wait_send()
            quarters(chunk, side).wait_send()
        back_across(chunk).wait_send()
        back_beside(chunk).wait_send()
        for k in range(3):
            shares(chunk, k).wait_send()
            back_around(chunk, k).wait_send()


def layer_kernel(*refs):
    w = Work(INPUTS + OUTPUTS + SCRATCH, refs)
    section = lax.axis_index("section")
    is_first = section == 0
    is_second = section == 1
    partner = {"section": 1 - section}
    micro = w.bnd.shape[0]

    def place_of(slot, index, half):
        row = (slot * micro + index) * PADDED + HALVES[half]["first"]
        return pl.ds(pl.multiple_of(row, 16), HALVES[half]["rows"])

    def load(index, half):
        span = pl.ds(HALVES[half]["first"], HALVES[half]["rows"])
        return pltpu.make_async_copy(
            w.bnd.at[index, span], w.buf.at[place_of(0, index, half)], w.load_sem.at[index, half]
        )

    def send(index, half):
        return pltpu.make_async_remote_copy(
            src_ref=w.stage.at[half, pl.ds(0, HALVES[half]["rows"])],
            dst_ref=w.buf.at[place_of(1, index, half)],
            send_sem=w.send_sem.at[index, half],
            recv_sem=w.recv_sem.at[index, half],
            device_id=partner,
            device_id_type=MESH,
        )

    def store(index, half):
        count = HALVES[half]["rows"]
        return pltpu.make_async_copy(
            w.kept.at[half, pl.ds(0, count)],
            w.res.at[index, pl.ds(HALVES[half]["first"], count)],
            w.out_sem.at[half],
        )

    barrier = pltpu.get_barrier_semaphore()
    group = Group() if lax.axis_size("dp") == 16 else None
    others = [partner] if group is None else [partner] + group.everyone
    for other in others:
        pl.semaphore_signal(barrier, inc=1, device_id=other, device_id_type=MESH)
    for index in range(micro):
        for half in range(2):
            load(index, half).start()
    clear_all(w)
    pl.semaphore_wait(barrier, len(others))

    def rows_of(slot, index, half):
        row = (slot * micro + index) * PADDED + HALVES[half]["first"]

        def read(at, size, columns=slice(None)):
            return w.buf[pl.ds(pl.multiple_of(row + at, 16), size), columns]

        return read

    def forward(step, index, half):
        rows = HALVES[half]["rows"]
        x_at = rows_of(section, index, half)
        entry_norm(w, half, x_at)
        lower_half(w, half)
        gate_norm(w, half)
        upper_half(w, half)
        mix(w, half)

        @pl.when(step < micro)
        def _():
            @pl.when(jnp.logical_and(is_second, step > 0))
            def _():
                store(index - 1, half).wait()

            @pl.when(jnp.logical_and(is_first, step > 0))
            def _():
                send(index - 1, half).wait_send()

            def keep(span, y):
                @pl.when(is_second)
                def _():
                    w.kept[half, 0:rows, span] = y.astype(BF)

                @pl.when(is_first)
                def _():
                    w.stage[half, 0:rows, span] = y.astype(BF)

            project(w, half, x_at, keep)

            @pl.when(is_second)
            def _():
                store(index, half).start()

            @pl.when(is_first)
            def _():
                send(index, half).start()

    def backward(step, index, half):
        x_at = rows_of(section, index, half)
        gy_at = rows_of(1 - section, index, half)
        cotangent(w, half, gy_at)
        narrow_total(w, half)
        split(w, half)
        unmix(w, half)
        spatial_total(w, half)
        gate_back(w, half)
        widen_total(w, half)
        pull(w, half)

        @pl.when(is_first)
        def _():
            @pl.when(step > micro)
            def _():
                store(index - 1, half).wait()

            def keep(span, gx):
                w.kept[half, span, :] = gx.astype(BF)

            entry_back(w, half, x_at, gy_at, keep)
            store(index, half).start()

        @pl.when(is_second)
        def _():
            @pl.when(step > 0)
            def _():
                send(index - 1, half).wait_send()

            def keep(span, gx):
                w.stage[half, span, :] = gx.astype(BF)

            entry_back(w, half, x_at, gy_at, keep)
            send(index, half).start()

    def one_step(step, carry):
        index = lax.rem(step, micro)
        for half in range(2):

            @pl.when(step < micro)
            def _():
                load(index, half).wait()

            @pl.when(is_second)
            def _():
                send(index, half).wait_recv()

            forward(step, index, half)

            @pl.when(jnp.logical_and(is_first, step >= micro))
            def _():
                send(index, half).wait_recv()

            @pl.when(jnp.logical_or(is_second, step >= micro))
            def _():
                backward(step, index, half)

        return carry

    lax.fori_loop(0, micro * (2 - section), one_step, 0)

    for half in range(2):
        store(micro - 1, half).wait()
        send(micro - 1, half).wait_send()

    if group is not None:
        for other in group.everyone:
            pl.semaphore_signal(w.ready, inc=1, device_id=other, device_id_type=MESH)
    pack(w)
    if group is None:
        whole = pltpu.make_async_copy(w.gh, w.packed, w.own_sem.at[0])
        whole.start()
        whole.wait()
    else:
        pl.semaphore_wait(w.ready, len(group.everyone))
        add_up(w, group)


def scratch_of(micro, width, hidden):
    gate, most = hidden // 2, HALVES[1]["rows"]
    return [
        pltpu.VMEM((width + ONES, hidden), F32),
        pltpu.VMEM((width, gate), F32),
        pltpu.VMEM((3, 208, 256), F32),
        pltpu.VMEM((2, 336, 384), F32),
        pltpu.VMEM((592, 128), F32),
        pltpu.VMEM((656, 128), F32),
        pltpu.VMEM((2, 8, gate), F32),
        pltpu.VMEM((3, 8, width), F32),
        pltpu.VMEM((2 * micro * PADDED, width), BF),
        pltpu.VMEM((TALL, width), BF),
        pltpu.VMEM((width + ONES, TALL), BF),
        pltpu.VMEM((TALL, width), BF),
        pltpu.VMEM((width, TALL), BF),
        pltpu.VMEM((most, gate), BF),
        pltpu.VMEM((704, gate), BF),
        pltpu.VMEM((TALL, gate), BF),
        pltpu.VMEM((704, gate), BF),
        pltpu.VMEM((most, gate), BF),
        pltpu.VMEM((most, gate), F32),
        pltpu.VMEM((PACKED, hidden), BF),
        pltpu.VMEM((2, most, width), BF),
        pltpu.VMEM((2, most, width), BF),
        pltpu.SemaphoreType.DMA((micro, 2)),
        pltpu.SemaphoreType.DMA((micro, 2)),
        pltpu.SemaphoreType.DMA((micro, 2)),
        pltpu.SemaphoreType.DMA((2,)),
        pltpu.SemaphoreType.REGULAR,
        pltpu.SemaphoreType.DMA((6, CHUNKS)),
        pltpu.SemaphoreType.DMA((6, CHUNKS)),
        pltpu.SemaphoreType.DMA((2, 3, CHUNKS)),
        pltpu.SemaphoreType.DMA((2, 3, CHUNKS)),
        pltpu.SemaphoreType.DMA((CHUNKS,)),
    ]


def outputs_of(micro, width, hidden):
    return (
        jax.ShapeDtypeStruct((micro, PADDED, width), BF),
        jax.ShapeDtypeStruct((PACKED, hidden), BF),
    )


def place(square, offset, rows, columns):
    count = square.shape[0]
    return jnp.pad(square, ((offset, rows - offset - count), (offset, columns - offset - count)))


def windows(squares):
    small, middle, large = squares
    first = place(small, 0, 208, 256) + place(small, P_SMALL, 208, 256)
    return (
        jnp.stack([first, place(middle, 8, 208, 256), place(middle, 12, 208, 256)]),
        jnp.stack([place(large, 0, 336, 384), place(large, 4, 336, 384)]),
    )


def shards(
    boundary,
    entry_gain,
    entry_shift,
    widen_weight,
    hidden_bias,
    gate_gain,
    gate_shift,
    spatial_weight,
    position_bias,
    narrow_weight,
    output_bias,
    crop_starts,
):
    micro, rows_dev, width = boundary.shape[1:]
    hidden = widen_weight.shape[-1]
    gate = hidden // 2
    starts = crop_starts[0]
    spatial = spatial_weight[0]
    position = position_bias[0]
    bnd = jnp.pad(boundary[0], ((0, 0), (0, PADDED - rows_dev), (0, 0)))
    counts = (P_SMALL, P_MID, P_LARGE)
    squares = [
        lax.dynamic_slice(spatial, (starts[k], starts[k]), (c, c)) for k, c in enumerate(counts)
    ]
    shifts = [lax.dynamic_slice(position, (starts[k],), (c,)) for k, c in enumerate(counts)]
    sp_a, sp_b = windows(squares)
    spt_a, spt_b = windows([item.T for item in squares])
    pos_a = jnp.concatenate([shifts[0], shifts[0], shifts[1], shifts[1]])
    pos_b = jnp.pad(jnp.concatenate([shifts[2], shifts[2]]), (0, 8))
    pos_a = jnp.broadcast_to(pos_a[:, None], (592, 128))
    pos_b = jnp.broadcast_to(pos_b[:, None], (656, 128))

    vmem = pl.BlockSpec(memory_space=pltpu.VMEM)
    anywhere = pl.BlockSpec(memory_space=pl.ANY)
    outs = pl.pallas_call(
        layer_kernel,
        out_shape=outputs_of(micro, width, hidden),
        in_specs=[anywhere] + [vmem] * 14,
        out_specs=[anywhere] * 2,
        scratch_shapes=scratch_of(micro, width, hidden),
        compiler_params=pltpu.CompilerParams(
            collective_id=0, has_side_effects=True, vmem_limit_bytes=int(63.9 * 2**20)
        ),
        name="layer_relay",
    )(
        bnd,
        widen_weight[0],
        narrow_weight[0],
        sp_a,
        sp_b,
        spt_a,
        spt_b,
        pos_a,
        pos_b,
        entry_gain,
        entry_shift,
        hidden_bias,
        gate_gain,
        gate_shift,
        output_bias,
    )
    results, packed = outs
    if lax.axis_size("dp") != 16:
        packed = lax.psum(packed.astype(F32), "dp").astype(BF)
    widen_grad = packed[:width].astype(F32)
    narrow_grad = jnp.concatenate(
        [packed[NARROW_AT:SMALL_AT, at : at + width] for at in range(0, hidden, width)]
    ).astype(F32)
    lines = packed[width : width + 3].astype(F32)
    hidden_grads = lines[0]
    gate_grads = lines[1].reshape(2, gate)
    entry_grads = lines[2, : 3 * width].reshape(3, width)
    strips = [packed[SMALL_AT:, at : at + width] for at in range(0, 5 * width, width)]
    upper, lower = jnp.concatenate(strips[:3]).astype(F32), jnp.concatenate(strips[3:]).astype(F32)

    def spread(block, count, start):
        most = P_LARGE - count
        padded = jnp.pad(block, [(most, most)] * block.ndim)
        return lax.dynamic_slice(padded, (most - start,) * block.ndim, (P_LARGE,) * block.ndim)

    spatial_total = (
        upper[:P_LARGE, :P_LARGE]
        + spread(upper[:P_SMALL, 384 : 384 + P_SMALL], P_SMALL, starts[0])
        + spread(lower[:P_MID, :P_MID], P_MID, starts[1])
    )
    position_total = (
        upper[:P_LARGE, 383]
        + spread(upper[:P_SMALL, 511], P_SMALL, starts[0])
        + spread(lower[:P_MID, 255], P_MID, starts[1])
    )
    return (
        results[None, :, :rows_dev].astype(F32),
        entry_grads[None],
        widen_grad[None],
        hidden_grads[None],
        gate_grads[None],
        spatial_total[None],
        position_total[None],
        narrow_grad[None],
    )


def solution(mesh):
    placed = (
        P("section", None, "dp", None),
        P("section", None),
        P("section", None),
        P("section", None, None),
        P("section", None),
        P("section", None),
        P("section", None),
        P("section", None, None),
        P("section", None),
        P("section", None, None),
        P("section", None),
        P("section", None),
    )
    return jax.shard_map(
        shards,
        mesh=mesh,
        in_specs=placed,
        out_specs=(
            P("section", None, "dp", None),
            P("section", None, None),
            P("section", None, None),
            P("section", None),
            P("section", None, None),
            P("section", None, None),
            P("section", None),
            P("section", None, None),
        ),
        check_vma=False,
    )
```

```python
import jax
import jax.numpy as jnp
from jax import lax
from jax.experimental import pallas as pl
from jax.experimental.pallas import tpu as pltpu
from jax.sharding import PartitionSpec as P

P_SMALL = 100
P_MID = 196
P_LARGE = 324
EPSILON = 1e-05
BF = jnp.bfloat16
F32 = jnp.float32
MESH = pl.DeviceIdType.MESH
TILE = 256
WIDE = 512
DEEP = 1536

HALVES = (
    {"first": 0, "rows": 592, "deep": 640, "starts": (0, 192, 384), "win": 208, "wide": 256, "out": 592},
    {"first": 592, "rows": 656, "deep": 768, "starts": (0, 320), "win": 336, "wide": 384, "out": 648},
)
PADDED = 1248
TALL = 768
PART = 32
NARROW_AT = 528
SMALL_AT = 784
SMALL = 112
PACKED = 896
CHUNKS = 7
ONES = 16


def dot(a, b):
    return lax.dot_general(a, b, (((1,), (0,)), ((), ())), preferred_element_type=F32)


def dot_nt(a, b):
    return lax.dot_general(a, b, (((1,), (1,)), ((), ())), preferred_element_type=F32)


def over_rows(rows, step, body, part=None):
    if part is not None:
        inner = body

        def body(at, size):
            for low in range(0, size, part):
                inner(at + low, min(part, size - low))

    def one(index, carry):
        body(pl.multiple_of(index * step, step), step)
        return carry

    if rows // step == 1:
        body(0, step)
    else:
        lax.fori_loop(0, rows // step, one, 0)
    if rows % step:
        body(rows - rows % step, rows % step)


def over_tiles(count, body, size=TILE, together=1):
    def one(index, carry):
        for k in range(together):
            body(pl.multiple_of(index * (size * together) + k * size, size))
        return carry

    if count == together:
        for k in range(together):
            body(k * size)
    else:
        lax.fori_loop(0, count // together, one, 0)


def fold8(values):
    rows = values.shape[0]
    total = values[0:8]
    for at in range(8, rows, 8):
        total = total + values[at : at + 8]
    return total


def assemble(parts, starts, rows):
    pieces = []
    win = parts[0].shape[0]
    for index, (part, start) in enumerate(zip(parts, starts)):
        low = 0
        if index > 0:
            low = starts[index - 1] + win - start
            pieces.append(parts[index - 1][win - low :] + part[:low])
        high = win if index == len(parts) - 1 else starts[index + 1] - start
        pieces.append(part[low:high])
    return jnp.concatenate(pieces, axis=0)


class Work:
    def __init__(self, names, refs):
        for name, ref in zip(names, refs):
            setattr(self, name, ref)


INPUTS = (
    "bnd", "widen", "narrow", "sp_a", "sp_b", "spt_a", "spt_b", "pos_a", "pos_b",
    "eg", "es", "hb", "gg", "gs", "ob",
)
OUTPUTS = ("res", "packed")
SCRATCH = (
    "wg", "ng", "ga", "gb", "pa", "pb", "gate_sum", "entry_sum",
    "buf", "n", "nt", "g", "gt", "u", "s", "m", "q", "z", "wide", "gh",
    "stage", "kept", "load_sem", "send_sem", "recv_sem", "out_sem",
    "ready", "across_send", "across_recv", "around_send", "around_recv", "own_sem",
)


def row_stats(x):
    centred = x - jnp.mean(x, axis=-1, keepdims=True)
    spread = jnp.mean(centred * centred, axis=-1, keepdims=True)
    return centred, lax.rsqrt(spread + EPSILON)


def entry_norm(w, half, x_at):
    spec = HALVES[half]

    def body(at, size):
        centred, factor = row_stats(x_at(at, size).astype(F32))
        w.n[pl.ds(at, size), :] = (centred * factor * w.eg[...] + w.es[...]).astype(BF)

    over_rows(spec["rows"], 336, body, PART)
    if spec["rows"] < HALVES[1]["rows"]:
        w.n[spec["rows"] : spec["deep"], :] = jnp.zeros((spec["deep"] - spec["rows"], w.n.shape[1]), BF)


def gelu_tile(w, rows, at):
    hidden = dot(w.n[0:rows, :], w.widen[:, pl.ds(at, TILE)]) + w.hb[:, pl.ds(at, TILE)]
    square = hidden * hidden
    curve = jnp.tanh(hidden * (0.7978845608028654 + 0.035677408136300125 * square))
    above = curve + 1.0
    active = (0.5 * hidden) * above
    slope = above * (0.5 + (hidden - active) * (0.7978845608028654 + 0.10703222440890037 * square))
    return active, slope


def lower_half(w, half):
    rows, gate = HALVES[half]["rows"], w.narrow.shape[0]

    def body(at):
        active, slope = gelu_tile(w, rows, gate + at)
        w.wide[0:rows, pl.ds(at, TILE)] = active
        w.gh[0:rows, pl.ds(gate + at, TILE)] = slope.astype(BF)

    over_tiles(gate // TILE, body, TILE, 6)


def gate_norm(w, half):
    gate = w.narrow.shape[0]

    def body(at, size):
        span = pl.ds(at, size)
        centred, factor = row_stats(w.wide[span, :])
        z = centred * factor
        w.z[span, :] = z.astype(BF)
        w.q[span, :] = (z * w.gg[...] + w.gs[...]).astype(BF)
        w.gh[span, gate:] = (w.gh[span, gate:].astype(F32) * factor).astype(BF)

    over_rows(HALVES[half]["rows"], 336, body, PART)


def upper_half(w, half):
    rows, gate = HALVES[half]["rows"], w.narrow.shape[0]

    def body(at):
        active, slope = gelu_tile(w, rows, at)
        w.u[0:rows, pl.ds(at, TILE)] = active.astype(BF)
        w.gh[0:rows, pl.ds(at, TILE)] = slope.astype(BF)

    over_tiles(gate // TILE, body, TILE, 6)


def mix(w, half):
    spec, gate = HALVES[half], w.narrow.shape[0]
    rows = spec["rows"]
    square, shift = (w.sp_a, w.sp_b)[half], (w.pos_a, w.pos_b)[half]

    def body(at):
        span = pl.ds(at, TILE)
        parts = [
            dot(square[i], w.q[start : start + spec["wide"], span])
            for i, start in enumerate(spec["starts"])
        ]
        line = shift[...]
        mixed = assemble(parts, spec["starts"], rows) + jnp.concatenate([line, line], axis=1)
        w.s[0:rows, span] = mixed.astype(BF)
        w.m[0:rows, span] = (w.u[0:rows, span].astype(F32) * mixed).astype(BF)

    over_tiles(gate // TILE, body, TILE, 6)


def project(w, half, x_at, keep):
    rows = HALVES[half]["rows"]

    def body(at):
        span = pl.ds(at, WIDE)
        y = dot(w.m[0:rows, :], w.narrow[:, span])
        keep(span, x_at(0, rows, span).astype(F32) + (y + w.ob[:, span]))

    over_tiles(w.narrow.shape[1] // WIDE, body, WIDE)


def cotangent(w, half, gy_at):
    spec = HALVES[half]
    rows, deep, width = spec["rows"], spec["deep"], w.narrow.shape[1]

    def body(at, size):
        g = gy_at(at, size)
        w.g[pl.ds(at, size), :] = g
        w.entry_sum[2] += fold8(g.astype(F32))

    over_rows(rows, rows, body)
    if rows < HALVES[1]["rows"]:
        w.g[rows:deep, :] = jnp.zeros((deep - rows, width), BF)
    w.gt[:, 0:deep] = w.g[0:deep, :].T
    w.nt[0:width, 0:deep] = w.n[0:deep, :].T
    lane = lax.broadcasted_iota(jnp.int32, (ONES, deep), 1)
    w.nt[width : width + ONES, 0:deep] = jnp.where(lane < rows, 1.0, 0.0).astype(BF)


def narrow_total(w, half):
    deep = HALVES[half]["deep"]

    def body(at):
        span = pl.ds(at, DEEP)
        w.ng[:, span] += dot(w.gt[:, 0:deep], w.m[0:deep, span])

    over_tiles(w.narrow.shape[0] // DEEP, body, DEEP)


def split(w, half):
    rows = HALVES[half]["rows"]
    line = (w.pa, w.pb)[half]

    def body(at):
        span = pl.ds(at, DEEP)
        gm = dot_nt(w.g[0:rows, :], w.narrow[span, :])
        moved = (gm * w.u[0:rows, span].astype(F32)).astype(BF)
        mixed = w.s[0:rows, span].astype(F32)
        w.s[0:rows, span] = moved
        moved = moved.astype(F32)
        line[...] += sum(moved[:, i : i + 128] for i in range(0, DEEP, 128))
        w.gh[0:rows, span] = (gm * mixed * w.gh[0:rows, span].astype(F32)).astype(BF)

    over_tiles(w.narrow.shape[0] // DEEP, body, DEEP)


def unmix(w, half):
    spec = HALVES[half]
    square = (w.spt_a, w.spt_b)[half]

    def body(at):
        span = pl.ds(at, TILE)
        parts = [
            dot(square[i], w.s[start : start + spec["wide"], span])
            for i, start in enumerate(spec["starts"])
        ]
        w.wide[0 : spec["rows"], span] = assemble(parts, spec["starts"], spec["rows"])

    over_tiles(w.narrow.shape[0] // TILE, body, TILE, 6)


def spatial_total(w, half):
    spec = HALVES[half]
    total = (w.ga, w.gb)[half]
    for i, start in enumerate(spec["starts"]):
        total[i] += dot_nt(w.s[start : start + spec["win"], :], w.q[start : start + spec["wide"], :])


def gate_back(w, half):
    gate = w.narrow.shape[0]

    def body(at, size):
        span = pl.ds(at, size)
        gq = w.wide[span, :]
        z = w.z[span, :].astype(F32)
        w.gate_sum[0] += fold8(gq * z)
        w.gate_sum[1] += fold8(gq)
        e = gq * w.gg[...]
        first_mean = jnp.mean(e, axis=-1, keepdims=True)
        second_mean = jnp.mean(e * z, axis=-1, keepdims=True)
        gv = (e - first_mean - z * second_mean) * w.gh[span, gate:].astype(F32)
        w.gh[span, gate : 2 * gate] = gv.astype(BF)

    over_rows(HALVES[half]["rows"], 336, body, PART)


def widen_total(w, half):
    deep = HALVES[half]["deep"]

    def body(at):
        span = pl.ds(at, DEEP)
        w.wg[:, span] += dot(w.nt[:, 0:deep], w.gh[0:deep, span])

    over_tiles(w.widen.shape[1] // DEEP, body, DEEP)


def pull(w, half):
    rows = HALVES[half]["rows"]

    def body(at):
        w.wide[0:rows, pl.ds(at, WIDE)] = dot_nt(w.gh[0:rows, :], w.widen[pl.ds(at, WIDE), :])

    over_tiles(w.widen.shape[0] // WIDE, body, WIDE)


def entry_back(w, half, x_at, gy_at, keep):
    width = w.widen.shape[0]

    def body(at, size):
        span = pl.ds(at, size)
        centred, factor = row_stats(x_at(at, size).astype(F32))
        z = centred * factor
        gn = w.wide[span, 0:width]
        w.entry_sum[0] += fold8(gn * z)
        w.entry_sum[1] += fold8(gn)
        e = gn * w.eg[...]
        first_mean = jnp.mean(e, axis=-1, keepdims=True)
        second_mean = jnp.mean(e * z, axis=-1, keepdims=True)
        keep(span, gy_at(at, size).astype(F32) + factor * (e - first_mean - z * second_mean))

    over_rows(HALVES[half]["rows"], 336, body, PART)


def clear(ref):
    def body(at, size):
        ref[pl.ds(at, size), :] = jnp.zeros((size, ref.shape[-1]), ref.dtype)

    over_rows(ref.shape[-2], 32, body)


def clear_all(w):
    for ref in (w.wg, w.ng, w.pa, w.pb, w.n, w.g, w.m, w.q, w.s, w.gh):
        clear(ref)
    for ref in (w.ga, w.gb, w.gate_sum, w.entry_sum):
        ref[...] = jnp.zeros(ref.shape, ref.dtype)


class Group:
    def __init__(self):
        at = lax.axis_index("dp")
        self.core = lax.rem(at, 2)
        self.x = lax.rem(at // 2, 2)
        self.z = at // 4
        self.beside = {"dp": at + 1 - 2 * self.core}
        self.across = {"dp": at + 2 - 4 * self.x}
        self.far = [lax.rem(self.z + off, 4) for off in (1, 2, 3)]
        self.around = [{"dp": far * 4 + lax.rem(at, 4)} for far in self.far]
        self.everyone = [self.beside, self.across] + self.around


def turn(values, rows, lanes):
    if rows:
        values = pltpu.roll(values, values.shape[0] - rows, 0)
    if lanes:
        values = pltpu.roll(values, values.shape[1] - lanes, 1)
    return values


def pack(w):
    gate, width = w.narrow.shape
    w.wg[width + 1 : width + 2, 0:gate] = jnp.sum(w.gate_sum[0], axis=0, keepdims=True)
    w.wg[width + 1 : width + 2, gate:] = jnp.sum(w.gate_sum[1], axis=0, keepdims=True)
    for k in range(3):
        w.wg[width + 2 : width + 3, k * width : (k + 1) * width] = jnp.sum(
            w.entry_sum[k], axis=0, keepdims=True
        )
    clear(w.gh.at[SMALL_AT:PACKED])

    def body(at, size):
        w.gh[pl.ds(at, size), :] = w.wg[pl.ds(at, size), :].astype(BF)

    over_rows(w.wg.shape[0], 48, body)
    for b in range(6):
        w.gh[NARROW_AT:SMALL_AT, b * 512 : (b + 1) * 512] = w.ng[:, b * 256 : (b + 1) * 256].T.astype(BF)

    def put(block, lane, first):
        for b in range(0, block.shape[0], SMALL):
            rows = block[b : b + SMALL]
            at = (first + b // SMALL) * 512 + lane
            w.gh[SMALL_AT : SMALL_AT + rows.shape[0], at : at + rows.shape[1]] = rows.astype(BF)

    def with_line(block, line):
        sums = jnp.sum(line[0 : block.shape[0]], axis=1, keepdims=True)
        last = lax.broadcasted_iota(jnp.int32, block.shape, 1) == block.shape[1] - 1
        return jnp.where(last, sums, block)

    line_a, line_b = w.pa[...], w.pb[...]
    large = w.gb[0] + turn(w.gb[1], 4, 4)
    put(with_line(large, line_b + turn(line_b, 324, 0)), 0, 0)
    small = (w.ga[0] + turn(w.ga[0], P_SMALL, P_SMALL))[:, 0:128]
    put(with_line(small, line_a + turn(line_a, P_SMALL, 0)), 384, 0)
    middle = turn(w.ga[1], 8, 8) + turn(w.ga[2], 12, 12)
    put(with_line(middle, turn(line_a, 200, 0) + turn(line_a, 396, 0)), 0, 3)


def add_up(w, group):
    part = PACKED // 4 // CHUNKS
    wide = w.gh.shape[1]
    sides = ((w.m, 0), (w.q, wide // 2))
    quarter = wide // 4

    def rows_at(core, chunk, x):
        return pl.multiple_of(core * (PACKED // 2) + (2 * chunk + x) * part, 16)

    def remote(src, dst, send, recv, to):
        return pltpu.make_async_remote_copy(
            src_ref=src, dst_ref=dst, send_sem=send, recv_sem=recv, device_id=to, device_id_type=MESH
        )

    def halves(chunk, side):
        land, column = sides[side]
        return remote(
            w.gh.at[pl.ds(rows_at(1 - group.core, chunk, 0), 2 * part), pl.ds(column, wide // 2)],
            land.at[pl.ds(2 * chunk * part, 2 * part)],
            w.across_send.at[side, chunk],
            w.across_recv.at[side, chunk],
            group.beside,
        )

    def quarters(chunk, side):
        land, column = sides[side]
        return remote(
            w.gh.at[pl.ds(rows_at(group.core, chunk, 1 - group.x), part), pl.ds(column, wide // 2)],
            land.at[pl.ds(PACKED // 2 + chunk * part, part)],
            w.across_send.at[2 + side, chunk],
            w.across_recv.at[2 + side, chunk],
            group.across,
        )

    def column_of(z):
        return pl.ds(pl.multiple_of(z * quarter, 128), quarter)

    def landed(chunk, k):
        row = (k // 2) * (PACKED // 4) + chunk * part
        return w.z.at[pl.ds(row, part), pl.ds((k % 2) * quarter, quarter)]

    def shares(chunk, k):
        return remote(
            w.gh.at[pl.ds(rows_at(group.core, chunk, group.x), part), column_of(group.far[k])],
            landed(chunk, k),
            w.around_send.at[0, k, chunk],
            w.around_recv.at[0, k, chunk],
            group.around[k],
        )

    def total_of(chunk):
        return w.u.at[pl.ds(chunk * part, part), pl.ds(0, quarter)]

    def own_place(chunk):
        return w.packed.at[pl.ds(rows_at(group.core, chunk, group.x), part), column_of(group.z)]

    def back_around(chunk, k):
        return remote(
            total_of(chunk),
            own_place(chunk),
            w.around_send.at[1, k, chunk],
            w.around_recv.at[1, k, chunk],
            group.around[k],
        )

    def own(chunk):
        return pltpu.make_async_copy(total_of(chunk), own_place(chunk), w.own_sem.at[chunk])

    def back_across(chunk):
        span = pl.ds(rows_at(group.core, chunk, group.x), part)
        return remote(
            w.packed.at[span],
            w.packed.at[span],
            w.across_send.at[4, chunk],
            w.across_recv.at[4, chunk],
            group.across,
        )

    def back_beside(chunk):
        span = pl.ds(rows_at(group.core, chunk, 0), 2 * part)
        return remote(
            w.packed.at[span],
            w.packed.at[span],
            w.across_send.at[5, chunk],
            w.across_recv.at[5, chunk],
            group.beside,
        )

    def accumulate(at, side, row, size):
        land, column = sides[side]
        rows, columns = pl.ds(at, size), pl.ds(column, wide // 2)
        total = w.gh[rows, columns].astype(F32) + land[row : row + size, :].astype(F32)
        w.gh[rows, columns] = total.astype(BF)

    def by_core(chunk):
        for side in range(2):
            halves(chunk, side).wait_recv()
            accumulate(rows_at(group.core, chunk, 0), side, 2 * chunk * part, 2 * part)
            quarters(chunk, side).start()

    def by_x(chunk):
        for side in range(2):
            quarters(chunk, side).wait_recv()
            accumulate(rows_at(group.core, chunk, group.x), side, PACKED // 2 + chunk * part, part)
        for k in range(3):
            shares(chunk, k).start()

    def by_z(chunk):
        total = w.gh[pl.ds(rows_at(group.core, chunk, group.x), part), column_of(group.z)].astype(F32)
        for k in range(3):
            shares(chunk, k).wait_recv()
            total = total + landed(chunk, k)[...].astype(F32)
        total_of(chunk)[...] = total.astype(BF)
        own(chunk).start()
        for k in range(3):
            back_around(chunk, k).start()

    def give_x(chunk):
        own(chunk).wait()
        for k in range(3):
            back_around(chunk, k).wait_recv()
        back_across(chunk).start()

    def give_core(chunk):
        back_across(chunk).wait_recv()
        back_beside(chunk).start()

    for chunk in range(CHUNKS):
        for side in range(2):
            halves(chunk, side).start()
    stages = (by_core, by_x, by_z, give_x, give_core)
    lags = (0, 1, 2, 3, 4)
    for turn_at in range(CHUNKS + lags[-1]):
        for stage, lag in zip(stages, lags):
            if 0 <= turn_at - lag < CHUNKS:
                stage(turn_at - lag)
    for chunk in range(CHUNKS):
        back_beside(chunk).wait_recv()
    for chunk in range(CHUNKS):
        for side in range(2):
            halves(chunk, side).wait_send()
            quarters(chunk, side).wait_send()
        back_across(chunk).wait_send()
        back_beside(chunk).wait_send()
        for k in range(3):
            shares(chunk, k).wait_send()
            back_around(chunk, k).wait_send()


def layer_kernel(*refs):
    w = Work(INPUTS + OUTPUTS + SCRATCH, refs)
    section = lax.axis_index("section")
    is_first = section == 0
    is_second = section == 1
    partner = {"section": 1 - section}
    micro = w.bnd.shape[0]

    def place_of(slot, index, half):
        row = (slot * micro + index) * PADDED + HALVES[half]["first"]
        return pl.ds(pl.multiple_of(row, 16), HALVES[half]["rows"])

    def load(index, half):
        span = pl.ds(HALVES[half]["first"], HALVES[half]["rows"])
        return pltpu.make_async_copy(
            w.bnd.at[index, span], w.buf.at[place_of(0, index, half)], w.load_sem.at[index, half]
        )

    def send(index, half):
        return pltpu.make_async_remote_copy(
            src_ref=w.stage.at[half, pl.ds(0, HALVES[half]["rows"])],
            dst_ref=w.buf.at[place_of(1, index, half)],
            send_sem=w.send_sem.at[index, half],
            recv_sem=w.recv_sem.at[index, half],
            device_id=partner,
            device_id_type=MESH,
        )

    def store(index, half):
        count = HALVES[half]["rows"]
        return pltpu.make_async_copy(
            w.kept.at[half, pl.ds(0, count)],
            w.res.at[index, pl.ds(HALVES[half]["first"], count)],
            w.out_sem.at[half],
        )

    barrier = pltpu.get_barrier_semaphore()
    group = Group() if lax.axis_size("dp") == 16 else None
    others = [partner] if group is None else [partner] + group.everyone
    for other in others:
        pl.semaphore_signal(barrier, inc=1, device_id=other, device_id_type=MESH)
    for index in range(micro):
        for half in range(2):
            load(index, half).start()
    clear_all(w)
    pl.semaphore_wait(barrier, len(others))

    def rows_of(slot, index, half):
        row = (slot * micro + index) * PADDED + HALVES[half]["first"]

        def read(at, size, columns=slice(None)):
            return w.buf[pl.ds(pl.multiple_of(row + at, 16), size), columns]

        return read

    def forward(step, index, half):
        rows = HALVES[half]["rows"]
        x_at = rows_of(section, index, half)
        entry_norm(w, half, x_at)
        lower_half(w, half)
        gate_norm(w, half)
        upper_half(w, half)
        mix(w, half)

        @pl.when(step < micro)
        def _():
            @pl.when(jnp.logical_and(is_second, step > 0))
            def _():
                store(index - 1, half).wait()

            @pl.when(jnp.logical_and(is_first, step > 0))
            def _():
                send(index - 1, half).wait_send()

            def keep(span, y):
                @pl.when(is_second)
                def _():
                    w.kept[half, 0:rows, span] = y.astype(BF)

                @pl.when(is_first)
                def _():
                    w.stage[half, 0:rows, span] = y.astype(BF)

            project(w, half, x_at, keep)

            @pl.when(is_second)
            def _():
                store(index, half).start()

            @pl.when(is_first)
            def _():
                send(index, half).start()

    def backward(step, index, half):
        x_at = rows_of(section, index, half)
        gy_at = rows_of(1 - section, index, half)
        cotangent(w, half, gy_at)
        narrow_total(w, half)
        split(w, half)
        unmix(w, half)
        spatial_total(w, half)
        gate_back(w, half)
        widen_total(w, half)
        pull(w, half)

        @pl.when(is_first)
        def _():
            @pl.when(step > micro)
            def _():
                store(index - 1, half).wait()

            def keep(span, gx):
                w.kept[half, span, :] = gx.astype(BF)

            entry_back(w, half, x_at, gy_at, keep)
            store(index, half).start()

        @pl.when(is_second)
        def _():
            @pl.when(step > 0)
            def _():
                send(index - 1, half).wait_send()

            def keep(span, gx):
                w.stage[half, span, :] = gx.astype(BF)

            entry_back(w, half, x_at, gy_at, keep)
            send(index, half).start()

    def one_step(step, carry):
        index = lax.rem(step, micro)
        for half in range(2):

            @pl.when(step < micro)
            def _():
                load(index, half).wait()

            @pl.when(is_second)
            def _():
                send(index, half).wait_recv()

            forward(step, index, half)

            @pl.when(jnp.logical_and(is_first, step >= micro))
            def _():
                send(index, half).wait_recv()

            @pl.when(jnp.logical_or(is_second, step >= micro))
            def _():
                backward(step, index, half)

        return carry

    lax.fori_loop(0, micro * (2 - section), one_step, 0)

    for half in range(2):
        store(micro - 1, half).wait()
        send(micro - 1, half).wait_send()

    if group is not None:
        for other in group.everyone:
            pl.semaphore_signal(w.ready, inc=1, device_id=other, device_id_type=MESH)
    pack(w)
    if group is None:
        whole = pltpu.make_async_copy(w.gh, w.packed, w.own_sem.at[0])
        whole.start()
        whole.wait()
    else:
        pl.semaphore_wait(w.ready, len(group.everyone))
        add_up(w, group)


def scratch_of(micro, width, hidden):
    gate, most = hidden // 2, HALVES[1]["rows"]
    return [
        pltpu.VMEM((width + ONES, hidden), F32),
        pltpu.VMEM((width, gate), F32),
        pltpu.VMEM((3, 208, 256), F32),
        pltpu.VMEM((2, 336, 384), F32),
        pltpu.VMEM((592, 128), F32),
        pltpu.VMEM((656, 128), F32),
        pltpu.VMEM((2, 8, gate), F32),
        pltpu.VMEM((3, 8, width), F32),
        pltpu.VMEM((2 * micro * PADDED, width), BF),
        pltpu.VMEM((TALL, width), BF),
        pltpu.VMEM((width + ONES, TALL), BF),
        pltpu.VMEM((TALL, width), BF),
        pltpu.VMEM((width, TALL), BF),
        pltpu.VMEM((most, gate), BF),
        pltpu.VMEM((704, gate), BF),
        pltpu.VMEM((TALL, gate), BF),
        pltpu.VMEM((704, gate), BF),
        pltpu.VMEM((most, gate), BF),
        pltpu.VMEM((most, gate), F32),
        pltpu.VMEM((PACKED, hidden), BF),
        pltpu.VMEM((2, most, width), BF),
        pltpu.VMEM((2, most, width), BF),
        pltpu.SemaphoreType.DMA((micro, 2)),
        pltpu.SemaphoreType.DMA((micro, 2)),
        pltpu.SemaphoreType.DMA((micro, 2)),
        pltpu.SemaphoreType.DMA((2,)),
        pltpu.SemaphoreType.REGULAR,
        pltpu.SemaphoreType.DMA((6, CHUNKS)),
        pltpu.SemaphoreType.DMA((6, CHUNKS)),
        pltpu.SemaphoreType.DMA((2, 3, CHUNKS)),
        pltpu.SemaphoreType.DMA((2, 3, CHUNKS)),
        pltpu.SemaphoreType.DMA((CHUNKS,)),
    ]


def outputs_of(micro, width, hidden):
    return (
        jax.ShapeDtypeStruct((micro, PADDED, width), BF),
        jax.ShapeDtypeStruct((PACKED, hidden), BF),
    )


def place(square, offset, rows, columns):
    count = square.shape[0]
    return jnp.pad(square, ((offset, rows - offset - count), (offset, columns - offset - count)))


def windows(squares):
    small, middle, large = squares
    first = place(small, 0, 208, 256) + place(small, P_SMALL, 208, 256)
    return (
        jnp.stack([first, place(middle, 8, 208, 256), place(middle, 12, 208, 256)]),
        jnp.stack([place(large, 0, 336, 384), place(large, 4, 336, 384)]),
    )


def shards(
    boundary,
    entry_gain,
    entry_shift,
    widen_weight,
    hidden_bias,
    gate_gain,
    gate_shift,
    spatial_weight,
    position_bias,
    narrow_weight,
    output_bias,
    crop_starts,
):
    micro, rows_dev, width = boundary.shape[1:]
    hidden = widen_weight.shape[-1]
    gate = hidden // 2
    starts = crop_starts[0]
    spatial = spatial_weight[0]
    position = position_bias[0]
    bnd = jnp.pad(boundary[0], ((0, 0), (0, PADDED - rows_dev), (0, 0)))
    counts = (P_SMALL, P_MID, P_LARGE)
    squares = [
        lax.dynamic_slice(spatial, (starts[k], starts[k]), (c, c)) for k, c in enumerate(counts)
    ]
    shifts = [lax.dynamic_slice(position, (starts[k],), (c,)) for k, c in enumerate(counts)]
    sp_a, sp_b = windows(squares)
    spt_a, spt_b = windows([item.T for item in squares])
    pos_a = jnp.concatenate([shifts[0], shifts[0], shifts[1], shifts[1]])
    pos_b = jnp.pad(jnp.concatenate([shifts[2], shifts[2]]), (0, 8))
    pos_a = jnp.broadcast_to(pos_a[:, None], (592, 128))
    pos_b = jnp.broadcast_to(pos_b[:, None], (656, 128))

    vmem = pl.BlockSpec(memory_space=pltpu.VMEM)
    anywhere = pl.BlockSpec(memory_space=pl.ANY)
    outs = pl.pallas_call(
        layer_kernel,
        out_shape=outputs_of(micro, width, hidden),
        in_specs=[anywhere] + [vmem] * 14,
        out_specs=[anywhere] * 2,
        scratch_shapes=scratch_of(micro, width, hidden),
        compiler_params=pltpu.CompilerParams(
            collective_id=0, has_side_effects=True, vmem_limit_bytes=int(63.9 * 2**20)
        ),
        name="layer_relay",
    )(
        bnd,
        widen_weight[0],
        narrow_weight[0],
        sp_a,
        sp_b,
        spt_a,
        spt_b,
        pos_a,
        pos_b,
        entry_gain,
        entry_shift,
        hidden_bias,
        gate_gain,
        gate_shift,
        output_bias,
    )
    results, packed = outs
    if lax.axis_size("dp") != 16:
        packed = lax.psum(packed.astype(F32), "dp").astype(BF)
    widen_grad = packed[:width].astype(F32)
    narrow_grad = jnp.concatenate(
        [packed[NARROW_AT:SMALL_AT, at : at + width] for at in range(0, hidden, width)]
    ).astype(F32)
    lines = packed[width : width + 3].astype(F32)
    hidden_grads = lines[0]
    gate_grads = lines[1].reshape(2, gate)
    entry_grads = lines[2, : 3 * width].reshape(3, width)
    strips = [packed[SMALL_AT:, at : at + width] for at in range(0, 5 * width, width)]
    upper, lower = jnp.concatenate(strips[:3]).astype(F32), jnp.concatenate(strips[3:]).astype(F32)

    def spread(block, count, start):
        most = P_LARGE - count
        padded = jnp.pad(block, [(most, most)] * block.ndim)
        return lax.dynamic_slice(padded, (most - start,) * block.ndim, (P_LARGE,) * block.ndim)

    spatial_total = (
        upper[:P_LARGE, :P_LARGE]
        + spread(upper[:P_SMALL, 384 : 384 + P_SMALL], P_SMALL, starts[0])
        + spread(lower[:P_MID, :P_MID], P_MID, starts[1])
    )
    position_total = (
        upper[:P_LARGE, 383]
        + spread(upper[:P_SMALL, 511], P_SMALL, starts[0])
        + spread(lower[:P_MID, 255], P_MID, starts[1])
    )
    return (
        results[None, :, :rows_dev].astype(F32),
        entry_grads[None],
        widen_grad[None],
        hidden_grads[None],
        gate_grads[None],
        spatial_total[None],
        position_total[None],
        narrow_grad[None],
    )


def solution(mesh):
    placed = (
        P("section", None, "dp", None),
        P("section", None),
        P("section", None),
        P("section", None, None),
        P("section", None),
        P("section", None),
        P("section", None),
        P("section", None, None),
        P("section", None),
        P("section", None, None),
        P("section", None),
        P("section", None),
    )
    return jax.shard_map(
        shards,
        mesh=mesh,
        in_specs=placed,
        out_specs=(
            P("section", None, "dp", None),
            P("section", None, None),
            P("section", None, None),
            P("section", None),
            P("section", None, None),
            P("section", None, None),
            P("section", None),
            P("section", None, None),
        ),
        check_vma=False,
    )
```

```python
import jax
import jax.numpy as jnp
from jax import lax
from jax.experimental import pallas as pl
from jax.experimental.pallas import tpu as pltpu
from jax.sharding import PartitionSpec as P

P_SMALL = 100
P_MID = 196
P_LARGE = 324
EPSILON = 1e-05
BF = jnp.bfloat16
F32 = jnp.float32
MESH = pl.DeviceIdType.MESH
TILE = 256
WIDE = 512
DEEP = 1536

HALVES = (
    {"first": 0, "rows": 592, "deep": 640, "starts": (0, 192, 384), "win": 208, "wide": 256, "out": 592},
    {"first": 592, "rows": 656, "deep": 768, "starts": (0, 320), "win": 336, "wide": 384, "out": 648},
)
PADDED = 1248
TALL = 768
PART = 32
NARROW_AT = 528
SMALL_AT = 784
SMALL = 112
PACKED = 896
CHUNKS = 7
ONES = 16


def dot(a, b):
    return lax.dot_general(a, b, (((1,), (0,)), ((), ())), preferred_element_type=F32)


def dot_nt(a, b):
    return lax.dot_general(a, b, (((1,), (1,)), ((), ())), preferred_element_type=F32)


def over_rows(rows, step, body, part=None):
    if part is not None:
        inner = body

        def body(at, size):
            for low in range(0, size, part):
                inner(at + low, min(part, size - low))

    def one(index, carry):
        body(pl.multiple_of(index * step, step), step)
        return carry

    if rows // step == 1:
        body(0, step)
    else:
        lax.fori_loop(0, rows // step, one, 0)
    if rows % step:
        body(rows - rows % step, rows % step)


def over_tiles(count, body, size=TILE, together=1):
    def one(index, carry):
        for k in range(together):
            body(pl.multiple_of(index * (size * together) + k * size, size))
        return carry

    if count == together:
        for k in range(together):
            body(k * size)
    else:
        lax.fori_loop(0, count // together, one, 0)


def fold8(values):
    rows = values.shape[0]
    total = values[0:8]
    for at in range(8, rows, 8):
        total = total + values[at : at + 8]
    return total


def assemble(parts, starts, rows):
    pieces = []
    win = parts[0].shape[0]
    for index, (part, start) in enumerate(zip(parts, starts)):
        low = 0
        if index > 0:
            low = starts[index - 1] + win - start
            pieces.append(parts[index - 1][win - low :] + part[:low])
        high = win if index == len(parts) - 1 else starts[index + 1] - start
        pieces.append(part[low:high])
    return jnp.concatenate(pieces, axis=0)


class Work:
    def __init__(self, names, refs):
        for name, ref in zip(names, refs):
            setattr(self, name, ref)


INPUTS = (
    "bnd", "widen", "narrow", "sp_a", "sp_b", "spt_a", "spt_b", "pos_a", "pos_b",
    "eg", "es", "hb", "gg", "gs", "ob",
)
OUTPUTS = ("res", "packed", "saved_u", "saved_z", "saved_upper", "saved_lower")
SAVED = ("u", "z", "upper", "lower")
SCRATCH = (
    "wg", "ng", "ga", "gb", "pa", "pb", "gate_sum", "entry_sum",
    "buf", "n", "nt", "g", "gt", "u", "s", "m", "q", "z", "wide", "gh",
    "stage", "kept", "load_sem", "send_sem", "recv_sem", "out_sem",
    "ready", "across_send", "across_recv", "around_send", "around_recv", "own_sem",
    "save_sem", "fetch_sem",
)


def row_stats(x):
    centred = x - jnp.mean(x, axis=-1, keepdims=True)
    spread = jnp.mean(centred * centred, axis=-1, keepdims=True)
    return centred, lax.rsqrt(spread + EPSILON)


def entry_norm(w, half, x_at):
    spec = HALVES[half]

    def body(at, size):
        centred, factor = row_stats(x_at(at, size).astype(F32))
        w.n[pl.ds(at, size), :] = (centred * factor * w.eg[...] + w.es[...]).astype(BF)

    over_rows(spec["rows"], 336, body, PART)
    if spec["rows"] < HALVES[1]["rows"]:
        w.n[spec["rows"] : spec["deep"], :] = jnp.zeros((spec["deep"] - spec["rows"], w.n.shape[1]), BF)


def gelu_tile(w, rows, at):
    hidden = dot(w.n[0:rows, :], w.widen[:, pl.ds(at, TILE)]) + w.hb[:, pl.ds(at, TILE)]
    square = hidden * hidden
    curve = jnp.tanh(hidden * (0.7978845608028654 + 0.035677408136300125 * square))
    above = curve + 1.0
    active = (0.5 * hidden) * above
    slope = above * (0.5 + (hidden - active) * (0.7978845608028654 + 0.10703222440890037 * square))
    return active, slope


def lower_half(w, half):
    rows, gate = HALVES[half]["rows"], w.narrow.shape[0]

    def body(at):
        active, slope = gelu_tile(w, rows, gate + at)
        w.wide[0:rows, pl.ds(at, TILE)] = active
        w.gh[0:rows, pl.ds(gate + at, TILE)] = slope.astype(BF)

    over_tiles(gate // TILE, body, TILE, 6)


def gate_norm(w, half):
    gate = w.narrow.shape[0]

    def body(at, size):
        span = pl.ds(at, size)
        centred, factor = row_stats(w.wide[span, :])
        z = centred * factor
        w.z[span, :] = z.astype(BF)
        w.q[span, :] = (z * w.gg[...] + w.gs[...]).astype(BF)
        w.gh[span, gate:] = (w.gh[span, gate:].astype(F32) * factor).astype(BF)

    over_rows(HALVES[half]["rows"], 336, body, PART)


def gate_again(w, half):
    def body(at, size):
        span = pl.ds(at, size)
        w.q[span, :] = (w.z[span, :].astype(F32) * w.gg[...] + w.gs[...]).astype(BF)

    over_rows(HALVES[half]["rows"], 336, body, PART)


def upper_half(w, half):
    rows, gate = HALVES[half]["rows"], w.narrow.shape[0]

    def body(at):
        active, slope = gelu_tile(w, rows, at)
        w.u[0:rows, pl.ds(at, TILE)] = active.astype(BF)
        w.gh[0:rows, pl.ds(at, TILE)] = slope.astype(BF)

    over_tiles(gate // TILE, body, TILE, 6)


def mix(w, half):
    spec, gate = HALVES[half], w.narrow.shape[0]
    rows = spec["rows"]
    square, shift = (w.sp_a, w.sp_b)[half], (w.pos_a, w.pos_b)[half]

    def body(at):
        span = pl.ds(at, TILE)
        parts = [
            dot(square[i], w.q[start : start + spec["wide"], span])
            for i, start in enumerate(spec["starts"])
        ]
        line = shift[...]
        mixed = assemble(parts, spec["starts"], rows) + jnp.concatenate([line, line], axis=1)
        w.s[0:rows, span] = mixed.astype(BF)
        w.m[0:rows, span] = (w.u[0:rows, span].astype(F32) * mixed).astype(BF)

    over_tiles(gate // TILE, body, TILE, 6)


def project(w, half, x_at, keep):
    rows = HALVES[half]["rows"]

    def body(at):
        span = pl.ds(at, WIDE)
        y = dot(w.m[0:rows, :], w.narrow[:, span])
        keep(span, x_at(0, rows, span).astype(F32) + (y + w.ob[:, span]))

    over_tiles(w.narrow.shape[1] // WIDE, body, WIDE)


def cotangent(w, half, gy_at):
    spec = HALVES[half]
    rows, deep, width = spec["rows"], spec["deep"], w.narrow.shape[1]

    def body(at, size):
        g = gy_at(at, size)
        w.g[pl.ds(at, size), :] = g
        w.entry_sum[2] += fold8(g.astype(F32))

    over_rows(rows, rows, body)
    if rows < HALVES[1]["rows"]:
        w.g[rows:deep, :] = jnp.zeros((deep - rows, width), BF)
    w.gt[:, 0:deep] = w.g[0:deep, :].T
    w.nt[0:width, 0:deep] = w.n[0:deep, :].T
    lane = lax.broadcasted_iota(jnp.int32, (ONES, deep), 1)
    w.nt[width : width + ONES, 0:deep] = jnp.where(lane < rows, 1.0, 0.0).astype(BF)


def narrow_total(w, half):
    deep = HALVES[half]["deep"]

    def body(at):
        span = pl.ds(at, DEEP)
        w.ng[:, span] += dot(w.gt[:, 0:deep], w.m[0:deep, span])

    over_tiles(w.narrow.shape[0] // DEEP, body, DEEP)


def split(w, half):
    rows = HALVES[half]["rows"]
    line = (w.pa, w.pb)[half]

    def body(at):
        span = pl.ds(at, DEEP)
        gm = dot_nt(w.g[0:rows, :], w.narrow[span, :])
        moved = (gm * w.u[0:rows, span].astype(F32)).astype(BF)
        mixed = w.s[0:rows, span].astype(F32)
        w.s[0:rows, span] = moved
        moved = moved.astype(F32)
        line[...] += sum(moved[:, i : i + 128] for i in range(0, DEEP, 128))
        w.gh[0:rows, span] = (gm * mixed * w.gh[0:rows, span].astype(F32)).astype(BF)

    over_tiles(w.narrow.shape[0] // DEEP, body, DEEP)


def unmix(w, half):
    spec = HALVES[half]
    square = (w.spt_a, w.spt_b)[half]

    def body(at):
        span = pl.ds(at, TILE)
        parts = [
            dot(square[i], w.s[start : start + spec["wide"], span])
            for i, start in enumerate(spec["starts"])
        ]
        w.wide[0 : spec["rows"], span] = assemble(parts, spec["starts"], spec["rows"])

    over_tiles(w.narrow.shape[0] // TILE, body, TILE, 6)


def spatial_total(w, half):
    spec = HALVES[half]
    total = (w.ga, w.gb)[half]
    for i, start in enumerate(spec["starts"]):
        total[i] += dot_nt(w.s[start : start + spec["win"], :], w.q[start : start + spec["wide"], :])


def gate_back(w, half):
    gate = w.narrow.shape[0]

    def body(at, size):
        span = pl.ds(at, size)
        gq = w.wide[span, :]
        z = w.z[span, :].astype(F32)
        w.gate_sum[0] += fold8(gq * z)
        w.gate_sum[1] += fold8(gq)
        e = gq * w.gg[...]
        first_mean = jnp.mean(e, axis=-1, keepdims=True)
        second_mean = jnp.mean(e * z, axis=-1, keepdims=True)
        gv = (e - first_mean - z * second_mean) * w.gh[span, gate:].astype(F32)
        w.gh[span, gate : 2 * gate] = gv.astype(BF)

    over_rows(HALVES[half]["rows"], 336, body, PART)


def widen_total(w, half):
    deep = HALVES[half]["deep"]

    def body(at):
        span = pl.ds(at, DEEP)
        w.wg[:, span] += dot(w.nt[:, 0:deep], w.gh[0:deep, span])

    over_tiles(w.widen.shape[1] // DEEP, body, DEEP)


def pull(w, half):
    rows = HALVES[half]["rows"]

    def body(at):
        w.wide[0:rows, pl.ds(at, WIDE)] = dot_nt(w.gh[0:rows, :], w.widen[pl.ds(at, WIDE), :])

    over_tiles(w.widen.shape[0] // WIDE, body, WIDE)


def entry_back(w, half, x_at, gy_at, keep):
    width = w.widen.shape[0]

    def body(at, size):
        span = pl.ds(at, size)
        centred, factor = row_stats(x_at(at, size).astype(F32))
        z = centred * factor
        gn = w.wide[span, 0:width]
        w.entry_sum[0] += fold8(gn * z)
        w.entry_sum[1] += fold8(gn)
        e = gn * w.eg[...]
        first_mean = jnp.mean(e, axis=-1, keepdims=True)
        second_mean = jnp.mean(e * z, axis=-1, keepdims=True)
        keep(span, gy_at(at, size).astype(F32) + factor * (e - first_mean - z * second_mean))

    over_rows(HALVES[half]["rows"], 336, body, PART)


def clear(ref):
    def body(at, size):
        ref[pl.ds(at, size), :] = jnp.zeros((size, ref.shape[-1]), ref.dtype)

    over_rows(ref.shape[-2], 32, body)


def clear_all(w):
    for ref in (w.wg, w.ng, w.pa, w.pb, w.n, w.g, w.m, w.q, w.s, w.gh):
        clear(ref)
    for ref in (w.ga, w.gb, w.gate_sum, w.entry_sum):
        ref[...] = jnp.zeros(ref.shape, ref.dtype)


class Group:
    def __init__(self):
        at = lax.axis_index("dp")
        self.core = lax.rem(at, 2)
        self.x = lax.rem(at // 2, 2)
        self.z = at // 4
        self.beside = {"dp": at + 1 - 2 * self.core}
        self.across = {"dp": at + 2 - 4 * self.x}
        self.far = [lax.rem(self.z + off, 4) for off in (1, 2, 3)]
        self.around = [{"dp": far * 4 + lax.rem(at, 4)} for far in self.far]
        self.everyone = [self.beside, self.across] + self.around


def turn(values, rows, lanes):
    if rows:
        values = pltpu.roll(values, values.shape[0] - rows, 0)
    if lanes:
        values = pltpu.roll(values, values.shape[1] - lanes, 1)
    return values


def pack(w):
    gate, width = w.narrow.shape
    w.wg[width + 1 : width + 2, 0:gate] = jnp.sum(w.gate_sum[0], axis=0, keepdims=True)
    w.wg[width + 1 : width + 2, gate:] = jnp.sum(w.gate_sum[1], axis=0, keepdims=True)
    for k in range(3):
        w.wg[width + 2 : width + 3, k * width : (k + 1) * width] = jnp.sum(
            w.entry_sum[k], axis=0, keepdims=True
        )
    clear(w.gh.at[SMALL_AT:PACKED])

    def body(at, size):
        w.gh[pl.ds(at, size), :] = w.wg[pl.ds(at, size), :].astype(BF)

    over_rows(w.wg.shape[0], 48, body)
    for b in range(6):
        w.gh[NARROW_AT:SMALL_AT, b * 512 : (b + 1) * 512] = w.ng[:, b * 256 : (b + 1) * 256].T.astype(BF)

    def put(block, lane, first):
        for b in range(0, block.shape[0], SMALL):
            rows = block[b : b + SMALL]
            at = (first + b // SMALL) * 512 + lane
            w.gh[SMALL_AT : SMALL_AT + rows.shape[0], at : at + rows.shape[1]] = rows.astype(BF)

    def with_line(block, line):
        sums = jnp.sum(line[0 : block.shape[0]], axis=1, keepdims=True)
        last = lax.broadcasted_iota(jnp.int32, block.shape, 1) == block.shape[1] - 1
        return jnp.where(last, sums, block)

    line_a, line_b = w.pa[...], w.pb[...]
    large = w.gb[0] + turn(w.gb[1], 4, 4)
    put(with_line(large, line_b + turn(line_b, 324, 0)), 0, 0)
    small = (w.ga[0] + turn(w.ga[0], P_SMALL, P_SMALL))[:, 0:128]
    put(with_line(small, line_a + turn(line_a, P_SMALL, 0)), 384, 0)
    middle = turn(w.ga[1], 8, 8) + turn(w.ga[2], 12, 12)
    put(with_line(middle, turn(line_a, 200, 0) + turn(line_a, 396, 0)), 0, 3)


def add_up(w, group):
    part = PACKED // 4 // CHUNKS
    wide = w.gh.shape[1]
    sides = ((w.m, 0), (w.q, wide // 2))
    quarter = wide // 4

    def rows_at(core, chunk, x):
        return pl.multiple_of(core * (PACKED // 2) + (2 * chunk + x) * part, 16)

    def remote(src, dst, send, recv, to):
        return pltpu.make_async_remote_copy(
            src_ref=src, dst_ref=dst, send_sem=send, recv_sem=recv, device_id=to, device_id_type=MESH
        )

    def halves(chunk, side):
        land, column = sides[side]
        return remote(
            w.gh.at[pl.ds(rows_at(1 - group.core, chunk, 0), 2 * part), pl.ds(column, wide // 2)],
            land.at[pl.ds(2 * chunk * part, 2 * part)],
            w.across_send.at[side, chunk],
            w.across_recv.at[side, chunk],
            group.beside,
        )

    def quarters(chunk, side):
        land, column = sides[side]
        return remote(
            w.gh.at[pl.ds(rows_at(group.core, chunk, 1 - group.x), part), pl.ds(column, wide // 2)],
            land.at[pl.ds(PACKED // 2 + chunk * part, part)],
            w.across_send.at[2 + side, chunk],
            w.across_recv.at[2 + side, chunk],
            group.across,
        )

    def column_of(z):
        return pl.ds(pl.multiple_of(z * quarter, 128), quarter)

    def landed(chunk, k):
        row = (k // 2) * (PACKED // 4) + chunk * part
        return w.z.at[pl.ds(row, part), pl.ds((k % 2) * quarter, quarter)]

    def shares(chunk, k):
        return remote(
            w.gh.at[pl.ds(rows_at(group.core, chunk, group.x), part), column_of(group.far[k])],
            landed(chunk, k),
            w.around_send.at[0, k, chunk],
            w.around_recv.at[0, k, chunk],
            group.around[k],
        )

    def total_of(chunk):
        return w.u.at[pl.ds(chunk * part, part), pl.ds(0, quarter)]

    def own_place(chunk):
        return w.packed.at[pl.ds(rows_at(group.core, chunk, group.x), part), column_of(group.z)]

    def back_around(chunk, k):
        return remote(
            total_of(chunk),
            own_place(chunk),
            w.around_send.at[1, k, chunk],
            w.around_recv.at[1, k, chunk],
            group.around[k],
        )

    def own(chunk):
        return pltpu.make_async_copy(total_of(chunk), own_place(chunk), w.own_sem.at[chunk])

    def back_across(chunk):
        span = pl.ds(rows_at(group.core, chunk, group.x), part)
        return remote(
            w.packed.at[span],
            w.packed.at[span],
            w.across_send.at[4, chunk],
            w.across_recv.at[4, chunk],
            group.across,
        )

    def back_beside(chunk):
        span = pl.ds(rows_at(group.core, chunk, 0), 2 * part)
        return remote(
            w.packed.at[span],
            w.packed.at[span],
            w.across_send.at[5, chunk],
            w.across_recv.at[5, chunk],
            group.beside,
        )

    def accumulate(at, side, row, size):
        land, column = sides[side]
        rows, columns = pl.ds(at, size), pl.ds(column, wide // 2)
        total = w.gh[rows, columns].astype(F32) + land[row : row + size, :].astype(F32)
        w.gh[rows, columns] = total.astype(BF)

    def by_core(chunk):
        for side in range(2):
            halves(chunk, side).wait_recv()
            accumulate(rows_at(group.core, chunk, 0), side, 2 * chunk * part, 2 * part)
            quarters(chunk, side).start()

    def by_x(chunk):
        for side in range(2):
            quarters(chunk, side).wait_recv()
            accumulate(rows_at(group.core, chunk, group.x), side, PACKED // 2 + chunk * part, part)
        for k in range(3):
            shares(chunk, k).start()

    def by_z(chunk):
        total = w.gh[pl.ds(rows_at(group.core, chunk, group.x), part), column_of(group.z)].astype(F32)
        for k in range(3):
            shares(chunk, k).wait_recv()
            total = total + landed(chunk, k)[...].astype(F32)
        total_of(chunk)[...] = total.astype(BF)
        own(chunk).start()
        for k in range(3):
            back_around(chunk, k).start()

    def give_x(chunk):
        own(chunk).wait()
        for k in range(3):
            back_around(chunk, k).wait_recv()
        back_across(chunk).start()

    def give_core(chunk):
        back_across(chunk).wait_recv()
        back_beside(chunk).start()

    for chunk in range(CHUNKS):
        for side in range(2):
            halves(chunk, side).start()
    stages = (by_core, by_x, by_z, give_x, give_core)
    lags = (0, 1, 2, 3, 4)
    for turn_at in range(CHUNKS + lags[-1]):
        for stage, lag in zip(stages, lags):
            if 0 <= turn_at - lag < CHUNKS:
                stage(turn_at - lag)
    for chunk in range(CHUNKS):
        back_beside(chunk).wait_recv()
    for chunk in range(CHUNKS):
        for side in range(2):
            halves(chunk, side).wait_send()
            quarters(chunk, side).wait_send()
        back_across(chunk).wait_send()
        back_beside(chunk).wait_send()
        for k in range(3):
            shares(chunk, k).wait_send()
            back_around(chunk, k).wait_send()


def layer_kernel(*refs):
    w = Work(INPUTS + OUTPUTS + SCRATCH, refs)
    section = lax.axis_index("section")
    is_first = section == 0
    is_second = section == 1
    partner = {"section": 1 - section}
    micro = w.bnd.shape[0]

    def place_of(slot, index, half):
        row = (slot * micro + index) * PADDED + HALVES[half]["first"]
        return pl.ds(pl.multiple_of(row, 16), HALVES[half]["rows"])

    def load(index, half):
        span = pl.ds(HALVES[half]["first"], HALVES[half]["rows"])
        return pltpu.make_async_copy(
            w.bnd.at[index, span], w.buf.at[place_of(0, index, half)], w.load_sem.at[index, half]
        )

    def send(index, half):
        return pltpu.make_async_remote_copy(
            src_ref=w.stage.at[half, pl.ds(0, HALVES[half]["rows"])],
            dst_ref=w.buf.at[place_of(1, index, half)],
            send_sem=w.send_sem.at[index, half],
            recv_sem=w.recv_sem.at[index, half],
            device_id=partner,
            device_id_type=MESH,
        )

    def store(index, half):
        count = HALVES[half]["rows"]
        return pltpu.make_async_copy(
            w.kept.at[half, pl.ds(0, count)],
            w.res.at[index, pl.ds(HALVES[half]["first"], count)],
            w.out_sem.at[half],
        )

    barrier = pltpu.get_barrier_semaphore()
    group = Group() if lax.axis_size("dp") == 16 else None
    others = [partner] if group is None else [partner] + group.everyone
    for other in others:
        pl.semaphore_signal(barrier, inc=1, device_id=other, device_id_type=MESH)
    for index in range(micro):
        for half in range(2):
            load(index, half).start()
    clear_all(w)
    pl.semaphore_wait(barrier, len(others))

    def rows_of(slot, index, half):
        row = (slot * micro + index) * PADDED + HALVES[half]["first"]

        def read(at, size, columns=slice(None)):
            return w.buf[pl.ds(pl.multiple_of(row + at, 16), size), columns]

        return read

    def saved(name, index, half):
        span = pl.ds(0, HALVES[half]["rows"])
        gate = w.narrow.shape[0]
        here = {
            "u": w.u.at[span],
            "z": w.z.at[span],
            "upper": w.gh.at[span, pl.ds(0, gate)],
            "lower": w.gh.at[span, pl.ds(gate, gate)],
        }
        return here[name], getattr(w, "saved_" + name).at[index, half, span]

    def save(name, index, half):
        here, there = saved(name, index, half)
        return pltpu.make_async_copy(here, there, w.save_sem.at[SAVED.index(name)])

    def fetch(name, index, half):
        here, there = saved(name, index, half)
        return pltpu.make_async_copy(there, here, w.fetch_sem.at[SAVED.index(name)])

    def before(index, half):
        return (index, 0) if half == 1 else (index - 1, 1)

    def forward(step, index, half):
        rows = HALVES[half]["rows"]
        x_at = rows_of(section, index, half)
        saves = is_first if half == 1 else jnp.logical_and(is_first, index > 0)

        def free(*names):
            @pl.when(saves)
            def _():
                for name in names:
                    save(name, *before(index, half)).wait()

        def put_away(*names):
            @pl.when(is_first)
            def _():
                for name in names:
                    save(name, index, half).start()

        entry_norm(w, half, x_at)

        @pl.when(step < micro)
        def _():
            free("lower")
            lower_half(w, half)
            free("z")
            gate_norm(w, half)
            put_away("z", "lower")
            free("u", "upper")
            upper_half(w, half)
            put_away("u", "upper")

        @pl.when(step >= micro)
        def _():
            fetch("z", index, half).wait()
            gate_again(w, half)
            fetch("u", index, half).wait()

        mix(w, half)

        @pl.when(step < micro)
        def _():
            @pl.when(jnp.logical_and(is_second, index > 0))
            def _():
                store(index - 1, half).wait()

            @pl.when(jnp.logical_and(is_first, index > 0))
            def _():
                send(index - 1, half).wait_send()

            def keep(span, y):
                @pl.when(is_second)
                def _():
                    w.kept[half, 0:rows, span] = y.astype(BF)

                @pl.when(is_first)
                def _():
                    w.stage[half, 0:rows, span] = y.astype(BF)

            project(w, half, x_at, keep)

            @pl.when(is_second)
            def _():
                store(index, half).start()

            @pl.when(is_first)
            def _():
                send(index, half).start()

    def backward(step, index, half):
        x_at = rows_of(section, index, half)
        gy_at = rows_of(1 - section, index, half)

        def need(*names):
            @pl.when(is_first)
            def _():
                for name in names:
                    fetch(name, index, half).wait()

        def done(*names):
            more = is_first if half == 0 else jnp.logical_and(is_first, index < micro - 1)

            @pl.when(more)
            def _():
                for name in names:
                    fetch(name, *((index, 1) if half == 0 else (index + 1, 0))).start()

        cotangent(w, half, gy_at)
        narrow_total(w, half)
        need("upper")
        split(w, half)
        done("u")
        unmix(w, half)
        spatial_total(w, half)
        need("lower")
        gate_back(w, half)
        done("z")
        widen_total(w, half)
        pull(w, half)
        done("upper", "lower")

        @pl.when(is_first)
        def _():
            @pl.when(step > micro)
            def _():
                store(index - 1, half).wait()

            def keep(span, gx):
                w.kept[half, span, :] = gx.astype(BF)

            entry_back(w, half, x_at, gy_at, keep)
            store(index, half).start()

        @pl.when(is_second)
        def _():
            @pl.when(step > 0)
            def _():
                send(index - 1, half).wait_send()

            def keep(span, gx):
                w.stage[half, span, :] = gx.astype(BF)

            entry_back(w, half, x_at, gy_at, keep)
            send(index, half).start()

    def one_step(step, carry):
        index = lax.rem(step, micro)

        @pl.when(jnp.logical_and(is_first, step == micro))
        def _():
            for name in SAVED:
                save(name, micro - 1, 1).wait()
                fetch(name, 0, 0).start()

        for half in range(2):

            @pl.when(step < micro)
            def _():
                load(index, half).wait()

                @pl.when(is_second)
                def _():
                    send(index, half).wait_recv()

            forward(step, index, half)

            @pl.when(jnp.logical_or(is_second, step >= micro))
            def _():
                @pl.when(is_first)
                def _():
                    send(index, half).wait_recv()

                backward(step, index, half)

        return carry

    lax.fori_loop(0, micro * (2 - section), one_step, 0)

    for half in range(2):
        store(micro - 1, half).wait()
        send(micro - 1, half).wait_send()

    if group is not None:
        for other in group.everyone:
            pl.semaphore_signal(w.ready, inc=1, device_id=other, device_id_type=MESH)
    pack(w)
    if group is None:
        whole = pltpu.make_async_copy(w.gh, w.packed, w.own_sem.at[0])
        whole.start()
        whole.wait()
    else:
        pl.semaphore_wait(w.ready, len(group.everyone))
        add_up(w, group)


def scratch_of(micro, width, hidden):
    gate, most = hidden // 2, HALVES[1]["rows"]
    return [
        pltpu.VMEM((width + ONES, hidden), F32),
        pltpu.VMEM((width, gate), F32),
        pltpu.VMEM((3, 208, 256), F32),
        pltpu.VMEM((2, 336, 384), F32),
        pltpu.VMEM((592, 128), F32),
        pltpu.VMEM((656, 128), F32),
        pltpu.VMEM((2, 8, gate), F32),
        pltpu.VMEM((3, 8, width), F32),
        pltpu.VMEM((2 * micro * PADDED, width), BF),
        pltpu.VMEM((TALL, width), BF),
        pltpu.VMEM((width + ONES, TALL), BF),
        pltpu.VMEM((TALL, width), BF),
        pltpu.VMEM((width, TALL), BF),
        pltpu.VMEM((most, gate), BF),
        pltpu.VMEM((704, gate), BF),
        pltpu.VMEM((TALL, gate), BF),
        pltpu.VMEM((704, gate), BF),
        pltpu.VMEM((most, gate), BF),
        pltpu.VMEM((most, gate), F32),
        pltpu.VMEM((PACKED, hidden), BF),
        pltpu.VMEM((2, most, width), BF),
        pltpu.VMEM((2, most, width), BF),
        pltpu.SemaphoreType.DMA((micro, 2)),
        pltpu.SemaphoreType.DMA((micro, 2)),
        pltpu.SemaphoreType.DMA((micro, 2)),
        pltpu.SemaphoreType.DMA((2,)),
        pltpu.SemaphoreType.REGULAR,
        pltpu.SemaphoreType.DMA((6, CHUNKS)),
        pltpu.SemaphoreType.DMA((6, CHUNKS)),
        pltpu.SemaphoreType.DMA((2, 3, CHUNKS)),
        pltpu.SemaphoreType.DMA((2, 3, CHUNKS)),
        pltpu.SemaphoreType.DMA((CHUNKS,)),
        pltpu.SemaphoreType.DMA((len(SAVED),)),
        pltpu.SemaphoreType.DMA((len(SAVED),)),
    ]


def outputs_of(micro, width, hidden):
    return (
        jax.ShapeDtypeStruct((micro, PADDED, width), BF),
        jax.ShapeDtypeStruct((PACKED, hidden), BF),
        *[jax.ShapeDtypeStruct((micro, 2, HALVES[1]["rows"], hidden // 2), BF)] * len(SAVED),
    )


def place(square, offset, rows, columns):
    count = square.shape[0]
    return jnp.pad(square, ((offset, rows - offset - count), (offset, columns - offset - count)))


def windows(squares):
    small, middle, large = squares
    first = place(small, 0, 208, 256) + place(small, P_SMALL, 208, 256)
    return (
        jnp.stack([first, place(middle, 8, 208, 256), place(middle, 12, 208, 256)]),
        jnp.stack([place(large, 0, 336, 384), place(large, 4, 336, 384)]),
    )


def shards(
    boundary,
    entry_gain,
    entry_shift,
    widen_weight,
    hidden_bias,
    gate_gain,
    gate_shift,
    spatial_weight,
    position_bias,
    narrow_weight,
    output_bias,
    crop_starts,
):
    micro, rows_dev, width = boundary.shape[1:]
    hidden = widen_weight.shape[-1]
    gate = hidden // 2
    starts = crop_starts[0]
    spatial = spatial_weight[0]
    position = position_bias[0]
    bnd = jnp.pad(boundary[0], ((0, 0), (0, PADDED - rows_dev), (0, 0)))
    counts = (P_SMALL, P_MID, P_LARGE)
    squares = [
        lax.dynamic_slice(spatial, (starts[k], starts[k]), (c, c)) for k, c in enumerate(counts)
    ]
    shifts = [lax.dynamic_slice(position, (starts[k],), (c,)) for k, c in enumerate(counts)]
    sp_a, sp_b = windows(squares)
    spt_a, spt_b = windows([item.T for item in squares])
    pos_a = jnp.concatenate([shifts[0], shifts[0], shifts[1], shifts[1]])
    pos_b = jnp.pad(jnp.concatenate([shifts[2], shifts[2]]), (0, 8))
    pos_a = jnp.broadcast_to(pos_a[:, None], (592, 128))
    pos_b = jnp.broadcast_to(pos_b[:, None], (656, 128))

    vmem = pl.BlockSpec(memory_space=pltpu.VMEM)
    anywhere = pl.BlockSpec(memory_space=pl.ANY)
    outs = pl.pallas_call(
        layer_kernel,
        out_shape=outputs_of(micro, width, hidden),
        in_specs=[anywhere] + [vmem] * 14,
        out_specs=[anywhere] * len(OUTPUTS),
        scratch_shapes=scratch_of(micro, width, hidden),
        compiler_params=pltpu.CompilerParams(
            collective_id=0, has_side_effects=True, vmem_limit_bytes=int(63.9 * 2**20)
        ),
        name="layer_relay",
    )(
        bnd,
        widen_weight[0],
        narrow_weight[0],
        sp_a,
        sp_b,
        spt_a,
        spt_b,
        pos_a,
        pos_b,
        entry_gain,
        entry_shift,
        hidden_bias,
        gate_gain,
        gate_shift,
        output_bias,
    )
    results, packed = outs[:2]
    if lax.axis_size("dp") != 16:
        packed = lax.psum(packed.astype(F32), "dp").astype(BF)
    widen_grad = packed[:width].astype(F32)
    narrow_grad = jnp.concatenate(
        [packed[NARROW_AT:SMALL_AT, at : at + width] for at in range(0, hidden, width)]
    ).astype(F32)
    lines = packed[width : width + 3].astype(F32)
    hidden_grads = lines[0]
    gate_grads = lines[1].reshape(2, gate)
    entry_grads = lines[2, : 3 * width].reshape(3, width)
    strips = [packed[SMALL_AT:, at : at + width] for at in range(0, 5 * width, width)]
    upper, lower = jnp.concatenate(strips[:3]).astype(F32), jnp.concatenate(strips[3:]).astype(F32)

    def spread(block, count, start):
        most = P_LARGE - count
        padded = jnp.pad(block, [(most, most)] * block.ndim)
        return lax.dynamic_slice(padded, (most - start,) * block.ndim, (P_LARGE,) * block.ndim)

    spatial_total = (
        upper[:P_LARGE, :P_LARGE]
        + spread(upper[:P_SMALL, 384 : 384 + P_SMALL], P_SMALL, starts[0])
        + spread(lower[:P_MID, :P_MID], P_MID, starts[1])
    )
    position_total = (
        upper[:P_LARGE, 383]
        + spread(upper[:P_SMALL, 511], P_SMALL, starts[0])
        + spread(lower[:P_MID, 255], P_MID, starts[1])
    )
    return (
        results[None, :, :rows_dev].astype(F32),
        entry_grads[None],
        widen_grad[None],
        hidden_grads[None],
        gate_grads[None],
        spatial_total[None],
        position_total[None],
        narrow_grad[None],
    )


def solution(mesh):
    placed = (
        P("section", None, "dp", None),
        P("section", None),
        P("section", None),
        P("section", None, None),
        P("section", None),
        P("section", None),
        P("section", None),
        P("section", None, None),
        P("section", None),
        P("section", None, None),
        P("section", None),
        P("section", None),
    )
    return jax.shard_map(
        shards,
        mesh=mesh,
        in_specs=placed,
        out_specs=(
            P("section", None, "dp", None),
            P("section", None, None),
            P("section", None, None),
            P("section", None),
            P("section", None, None),
            P("section", None, None),
            P("section", None),
            P("section", None, None),
        ),
        check_vma=False,
    )
```
